32 devices in a mesh: member: 4 (over z), row: 4 (over y, core), col: 2 (over x).
Axes of the slice: x: 2, y: 2, z: 4, core: 2. Of those that a mesh axis runs over, the one named last changes fastest.
Arguments:
- pert: bfloat16 [4, 3, 2, 64, 1024], P('member', None, None, 'row', 'col'), may hold values from -6 to 6
- probes: bfloat16 [4, 3, 2, 64, 1024], P('member', None, None, 'row', 'col'), may hold values from -6 to 6
- diff_class: int32 [64, 1024], P('row', 'col'), may hold values from 0 to 7
- class_rate: float32 [8], replicated, may hold values from 0.03 to 0.24
Outputs:
- cov_probe: float32 [4, 3, 2, 64, 1024], P('member', None, None, 'row', 'col')
The draws below stay inside these ranges and needn't reach their ends.
All inputs are finite; a program needn't handle non-finite values.
Results may differ from the reference program's by a relative error of at most 0.0018.
Values may be sent and summed in bfloat16 or wider, within the bound.
A program may use at most 128 MiB of HBM per device.

```python
import jax
import jax.numpy as jnp
from jax import lax

LEV = 2
VARS = 3
SWEEPS = 4
NCLASS = 8
MEMBERS = 4
PROBES = 4
NY = 64
NX = 1024


def plant(values, stream_key, least, largest):
    longest = values.shape.index(max(values.shape))
    spots = []
    for shift in (0, 1):
        where = [jax.random.randint(jax.random.fold_in(stream_key, axis), (), 0, length) for axis, length in enumerate(values.shape)]
        where[longest] = (where[longest] + shift) % values.shape[longest]
        spots.append(tuple(where))
    return values.at[spots[0]].set(least).at[spots[1]].set(largest)


def block_scale(stream_key, dims, split, low, largest):
    def one(axis_at, blocks):
        steps = jax.random.uniform(jax.random.fold_in(jax.random.fold_in(stream_key, 6), axis_at), (blocks,), jnp.float32, low / len(split), largest / len(split))
        return jnp.repeat(jnp.exp(steps), dims[axis_at] // blocks).reshape((-1,) + (1,) * (len(dims) - axis_at - 1))

    gain = one(*split[0])
    for cut in split[1:]:
        gain = gain * one(*cut)
    return gain


def centred(stream_key, shape, spread, limit, pieces=(), held_as=jnp.bfloat16):
    level = block_scale(stream_key, shape, pieces, -0.22, 0.18) if pieces else 1.0
    entries = jax.random.normal(stream_key, shape, jnp.float32) * spread * level
    return jnp.minimum(jnp.maximum(entries, -limit), limit).astype(held_as)


def setup_inputs(seed: int = 0) -> dict:
    key_list = jax.random.split(jax.random.key(seed), 5)
    return {
        "pert": centred(key_list[0], (MEMBERS, VARS, LEV, NY, NX), 1.0, 6.0, ((0, 4), (3, 4), (4, 2))),
        "probes": centred(key_list[1], (PROBES, VARS, LEV, NY, NX), 1.0, 6.0, ((0, 4), (3, 4), (4, 2))),
        "diff_class": plant(jax.random.randint(key_list[2], (NY, NX), 0, NCLASS), jax.random.fold_in(key_list[2], 1), 0, NCLASS - 1).astype(jnp.int32),
        "class_rate": jnp.clip(jax.random.uniform(key_list[3], (NCLASS,), jnp.float32, 0.03, 0.24), 0.03, 0.24),
    }


def class_rates(diff_class, class_rate):
    levels = jnp.arange(class_rate.shape[0], dtype=jnp.int32)
    picked = (diff_class[..., None] == levels).astype(jnp.float32)
    return jnp.sum(picked * class_rate.astype(jnp.float32), axis=-1)


def diffuse(field_now, cell_rate):
    widths = ((0, 0),) * (field_now.ndim - 2) + ((1, 1), (1, 1))
    padded = jnp.pad(field_now, widths)
    beside_all = padded[..., 2:, 1:-1] + padded[..., :-2, 1:-1] + padded[..., 1:-1, 2:] + padded[..., 1:-1, :-2]
    return field_now + cell_rate * (beside_all - 4.0 * field_now)


def reference(pert, probes, diff_class, class_rate):
    cell_rate = class_rates(diff_class, class_rate)
    probe_field = probes.astype(jnp.float32)

    def one_member(running, member):
        member_field = member.astype(jnp.float32)
        field_now = member_field[None] * probe_field
        for sweep_index in range(SWEEPS):
            field_now = diffuse(field_now, cell_rate)
        return running + member_field[None] * field_now, None

    running, unused = lax.scan(one_member, jnp.zeros(probe_field.shape, jnp.float32), pert)
    return running / (MEMBERS - 1)
```

```python
import functools

import jax
import jax.numpy as jnp
from jax import lax
from jax.experimental import pallas as pl
from jax.experimental.pallas import tpu as pltpu
from jax.sharding import PartitionSpec as P

SWEEPS = 4
MESH = pl.DeviceIdType.MESH
F32 = jnp.float32


def kernel(
    n, rows, cols,
    pert, probes, classes, rates, out,
    core, above, below, side, side_above, side_below,
    side_out, side_in, cls, cls_in, cls_above, cls_below,
    probe_field, keep, rate,
    z_send, z_recv, zs_send, zs_recv, y_send, y_recv, ys_send, ys_recv,
    x_send, x_recv, cx_send, cx_recv, cy_send, cy_recv,
):
    slabs, tile_rows, tile_cols = pert.shape
    pairs = slabs // 2
    half = tile_rows // 2
    wide = tile_cols + 128
    tall = tile_rows + half
    me = lax.axis_index("member")
    row = lax.axis_index("row")
    col = lax.axis_index("col")
    upper = (2 * me) // n

    def peer(step):
        mine = upper * (n - 1) + (1 - 2 * upper) * me
        other = step + (step + n - mine) // n
        return upper * (n - 1) + (1 - 2 * upper) * other

    has_up = (row + rows - 1) // rows
    has_down = 1 - (row + 1) // rows
    has_left = (col + cols - 1) // cols
    has_right = 1 - (col + 1) // cols
    sides = (
        (has_up, {"row": row - 1}),
        (has_down, {"row": row + 1}),
        (has_left, {"col": col - 1}),
        (has_right, {"col": col + 1}),
    )

    barrier = pltpu.get_barrier_semaphore()

    @pl.loop(0, n - 1)
    def _(step):
        pl.semaphore_signal(barrier, inc=1, device_id={"member": peer(step)}, device_id_type=MESH)

    for has, where in sides:
        @pl.when(has == 1)
        def _(where=where):
            pl.semaphore_signal(barrier, inc=1, device_id=where, device_id_type=MESH)

    def remote(src, dst, send, recv, where):
        return pltpu.make_async_remote_copy(
            src_ref=src, dst_ref=dst, send_sem=send, recv_sem=recv,
            device_id=where, device_id_type=MESH,
        )

    for which, slot in ((pert, me), (probes, n)):
        for pair in range(pairs):
            first = which[2 * pair].astype(F32)
            second = which[2 * pair + 1].astype(F32)
            for part in range(2):
                cut = slice(part * half, (part + 1) * half)
                core[slot, pair, part] = jnp.concatenate([first[cut], second[cut]], 0).astype(jnp.bfloat16)
    lane = lax.broadcasted_iota(jnp.int32, (tile_rows, 128), 1)
    for at, which in enumerate((pert, probes)):
        to_left = jnp.zeros((tile_rows, 128), F32)
        to_right = jnp.zeros((tile_rows, 128), F32)
        for slab in range(slabs):
            low = SWEEPS * slab
            head = which[slab, :, 0:128].astype(F32)
            tail = which[slab, :, tile_cols - 128 : tile_cols].astype(F32)
            if slab:
                head = pltpu.roll(head, low, 1)
                tail = pltpu.roll(tail, 128 - low, 1)
            to_left = jnp.where((lane >= low) & (lane < low + SWEEPS), head, to_left)
            to_right = jnp.where((lane >= 128 - SWEEPS - low) & (lane < 128 - low), tail, to_right)
        side_out[0, at] = to_left.astype(jnp.bfloat16)
        side_out[1, at] = to_right.astype(jnp.bfloat16)
    cls[:, 0:tile_cols] = classes[...]

    @pl.when(has_up == 0)
    def _():
        above[...] = jnp.zeros_like(above)
        side_above[...] = jnp.zeros_like(side_above)
        cls_above[...] = jnp.full_like(cls_above, -1)

    @pl.when(has_down == 0)
    def _():
        below[...] = jnp.zeros_like(below)
        side_below[...] = jnp.zeros_like(side_below)
        cls_below[...] = jnp.full_like(cls_below, -1)

    @pl.when(has_right == 0)
    def _():
        side_in[0] = jnp.zeros_like(side_in[0])
        cls_in[0] = jnp.full_like(cls_in[0], -1)

    @pl.when(has_left == 0)
    def _():
        side_in[1] = jnp.zeros_like(side_in[1])
        cls_in[1] = jnp.full_like(cls_in[1], -1)

    pl.semaphore_wait(barrier, n - 1 + has_up + has_down + has_left + has_right)

    def x_copies(at):
        where = sides[2 + at][1]
        block = (0, tile_cols - 128)[at]
        return (
            remote(side_out.at[at], side_in.at[at], x_send.at[at], x_recv.at[at], where),
            remote(classes.at[:, block : block + 128], cls_in.at[at], cx_send.at[at], cx_recv.at[at], where),
        )

    def z_copy(step):
        return remote(core.at[me], core.at[me], z_send.at[step], z_recv.at[me], {"member": peer(step)})

    def z_arrival(other):
        return remote(core.at[other], core.at[other], z_send.at[0], z_recv.at[other], {"member": other})

    def zs_copy(step):
        return remote(side.at[me], side.at[me], zs_send.at[step], zs_recv.at[me], {"member": peer(step)})

    def zs_arrival(other):
        return remote(side.at[other], side.at[other], zs_send.at[0], zs_recv.at[other], {"member": other})

    def y_copy(slot, at):
        return remote(
            core.at[slot, :, at], (below, above)[at].at[slot],
            y_send.at[slot, at], y_recv.at[slot, at], sides[at][1],
        )

    def ys_copy(slot, at):
        return remote(
            side.at[slot], (side_below, side_above)[at].at[slot],
            ys_send.at[slot, at], ys_recv.at[slot, at], sides[at][1],
        )

    def cy_copy(at):
        return remote(
            cls.at[at * half : (at + 1) * half], (cls_below, cls_above)[at],
            cy_send.at[at], cy_recv.at[at], sides[at][1],
        )

    def if_sent(at):
        return pl.when(sides[at][0] == 1)

    for at in range(2):
        @if_sent(2 + at)
        def _(at=at):
            for copy in x_copies(at):
                copy.start()

    @pl.loop(0, n - 1)
    def _(step):
        z_copy(step).start()

    for slot in (n, me):
        for at in range(2):
            @if_sent(at)
            def _(slot=slot, at=at):
                y_copy(slot, at).start()

    for at in range(2):
        @if_sent(3 - at)
        def _(at=at):
            for copy in x_copies(at):
                copy.wait_recv()

    for at, slot in enumerate((me, n)):
        merged = jnp.where(lane < 64, side_in[0, at].astype(F32), side_in[1, at].astype(F32))
        side[slot] = merged.astype(jnp.bfloat16)
    cls[:, tile_cols:wide] = jnp.where(lane < 64, cls_in[0], cls_in[1])

    for slot in (n, me):
        for at in range(2):
            @if_sent(at)
            def _(slot=slot, at=at):
                ys_copy(slot, at).start()

    for at in range(2):
        @if_sent(at)
        def _(at=at):
            cy_copy(at).start()

    @pl.loop(0, n - 1)
    def _(step):
        zs_copy(step).start()

    low_rows = lax.broadcasted_iota(jnp.int32, (2 * half, tile_cols), 0) % half < half // 2
    low_side = lax.broadcasted_iota(jnp.int32, (half, 128), 0) < half // 2
    lane_tall = lax.broadcasted_iota(jnp.int32, (tall, 128), 1) < 64

    def widened(slot, pair):
        head = core[slot, pair, 0].astype(F32)
        tail = core[slot, pair, 1].astype(F32)
        rim = jnp.where(low_rows, below[slot, pair].astype(F32), above[slot, pair].astype(F32))
        side_rim = jnp.where(
            low_side,
            side_below[slot].astype(F32)[0:half],
            side_above[slot].astype(F32)[half : 2 * half],
        )
        beside = jnp.concatenate([side[slot].astype(F32), side_rim], 0)
        both = []
        for at in range(2):
            low = SWEEPS * (2 * pair + at)
            cut = slice(at * half, (at + 1) * half)
            mine = jnp.concatenate([head[cut], tail[cut], rim[cut]], 0)
            end = jnp.where(
                lane_tall,
                pltpu.roll(beside, lax.rem(128 - low, 128), 1),
                pltpu.roll(beside, low, 1),
            )
            both.append(jnp.concatenate([mine, end], 1))
        return both

    def y_arrivals(slot):
        for at in range(2):
            @if_sent(1 - at)
            def _(at=at):
                y_copy(slot, at).wait_recv()
                ys_copy(slot, at).wait_recv()

    for at in range(2):
        @if_sent(1 - at)
        def _(at=at):
            cy_copy(at).wait_recv()

    low_cls = lax.broadcasted_iota(jnp.int32, (half, wide), 0) < half // 2
    kind = jnp.concatenate([cls[...], jnp.where(low_cls, cls_below[...], cls_above[...])], 0)
    picked = jnp.zeros((tall, wide), F32)
    for level in range(rates.shape[0]):
        picked = jnp.where(kind == level, rates[level], picked)
    rate[...] = picked
    keep[...] = 1.0 - 4.0 * picked

    y_arrivals(n)

    @pl.loop(0, pairs)
    def _(pair):
        for at, field in enumerate(widened(n, pair)):
            probe_field[2 * pair + at] = field * (1.0 / (n - 1))

    def add_member(slot, first):
        @pl.loop(0, pairs)
        def _(pair):
            for at, member in enumerate(widened(slot, pair)):
                slab = 2 * pair + at
                field = member * probe_field[slab]
                for _ in range(SWEEPS):
                    beside = (
                        pltpu.roll(field, 1, 0) + pltpu.roll(field, tall - 1, 0)
                        + pltpu.roll(field, 1, 1) + pltpu.roll(field, wide - 1, 1)
                    )
                    field = keep[...] * field + rate[...] * beside
                term = member[0:tile_rows, 0:tile_cols] * field[0:tile_rows, 0:tile_cols]
                out[slab] = term if first else out[slab] + term

    y_arrivals(me)
    add_member(me, True)

    @pl.loop(0, n - 1)
    def _(step):
        other = peer(step)
        z_arrival(other).wait_recv()
        for at in range(2):
            @if_sent(at)
            def _(at=at):
                y_copy(other, at).start()
        zs_arrival(other).wait_recv()
        for at in range(2):
            @if_sent(at)
            def _(at=at):
                ys_copy(other, at).start()
        y_arrivals(other)
        add_member(other, False)

    @pl.loop(0, n - 1)
    def _(step):
        z_copy(step).wait_send()
        zs_copy(step).wait_send()

    @pl.loop(0, n + 1)
    def _(slot):
        for at in range(2):
            @if_sent(at)
            def _(at=at):
                y_copy(slot, at).wait_send()
                ys_copy(slot, at).wait_send()

    for at in range(2):
        @if_sent(at)
        def _(at=at):
            cy_copy(at).wait_send()

        @if_sent(2 + at)
        def _(at=at):
            for copy in x_copies(at):
                copy.wait_send()


def body(n, rows, cols, pert, probes, diff_class, class_rate):
    mem_local, variables, levels, tile_rows, tile_cols = pert.shape
    slabs = variables * levels
    pairs = slabs // 2
    half = tile_rows // 2
    wide = tile_cols + 128
    tall = tile_rows + half
    bf16 = jnp.bfloat16
    flat = (slabs, tile_rows, tile_cols)
    vmem = pl.BlockSpec(memory_space=pltpu.VMEM)
    dma = pltpu.SemaphoreType.DMA
    out = pl.pallas_call(
        functools.partial(kernel, n, rows, cols),
        out_shape=jax.ShapeDtypeStruct(flat, F32),
        in_specs=[vmem, vmem, vmem, pl.BlockSpec(memory_space=pltpu.SMEM)],
        out_specs=vmem,
        scratch_shapes=[
            pltpu.VMEM((n + 1, pairs, 2, tile_rows, tile_cols), bf16),
            pltpu.VMEM((n + 1, pairs, tile_rows, tile_cols), bf16),
            pltpu.VMEM((n + 1, pairs, tile_rows, tile_cols), bf16),
            pltpu.VMEM((n + 1, tile_rows, 128), bf16),
            pltpu.VMEM((n + 1, tile_rows, 128), bf16),
            pltpu.VMEM((n + 1, tile_rows, 128), bf16),
            pltpu.VMEM((2, 2, tile_rows, 128), bf16),
            pltpu.VMEM((2, 2, tile_rows, 128), bf16),
            pltpu.VMEM((tile_rows, wide), jnp.int32),
            pltpu.VMEM((2, tile_rows, 128), jnp.int32),
            pltpu.VMEM((half, wide), jnp.int32),
            pltpu.VMEM((half, wide), jnp.int32),
            pltpu.VMEM((slabs, tall, wide), F32),
            pltpu.VMEM((tall, wide), F32),
            pltpu.VMEM((tall, wide), F32),
            dma((n,)), dma((n,)), dma((n,)), dma((n,)),
            dma((n + 1, 2)), dma((n + 1, 2)), dma((n + 1, 2)), dma((n + 1, 2)),
            dma((2,)), dma((2,)), dma((2,)), dma((2,)), dma((2,)), dma((2,)),
        ],
        compiler_params=pltpu.CompilerParams(
            collective_id=0, has_side_effects=True, vmem_limit_bytes=48 * 1024 * 1024
        ),
    )(pert.reshape(flat), probes.reshape(flat), diff_class, class_rate)
    return out.reshape(pert.shape)


def solution(mesh):
    placed = (
        P("member", None, None, "row", "col"),
        P("member", None, None, "row", "col"),
        P("row", "col"),
        P(),
    )
    sizes = (mesh.shape["member"], mesh.shape["row"], mesh.shape["col"])
    return jax.shard_map(
        functools.partial(body, *sizes),
        mesh=mesh,
        in_specs=placed,
        out_specs=P("member", None, None, "row", "col"),
        check_vma=False,
    )
```

```python
import functools

import jax
import jax.numpy as jnp
from jax import lax
from jax.experimental import pallas as pl
from jax.experimental.pallas import tpu as pltpu
from jax.sharding import PartitionSpec as P

SWEEPS = 4
MESH = pl.DeviceIdType.MESH
F32 = jnp.float32


def kernel(
    n, rows, cols,
    pert_hbm, probes_hbm, classes_hbm, rates_hbm, out,
    pert, probes, classes, rates,
    core, above, below, side, side_above, side_below,
    side_out, side_in, cls, cls_in, cls_above, cls_below,
    probe_field, keep, rate,
    in_sem, z_send, z_recv, zs_send, zs_recv, y_send, y_recv, ys_send, ys_recv,
    x_send, x_recv, cx_send, cx_recv, cy_send, cy_recv,
):
    slabs, tile_rows, tile_cols = pert.shape
    pairs = slabs // 2
    half = tile_rows // 2
    wide = tile_cols + 128
    tall = tile_rows + half
    me = lax.axis_index("member")
    row = lax.axis_index("row")
    col = lax.axis_index("col")

    loads = [
        pltpu.make_async_copy(src, dst, in_sem.at[at])
        for at, (src, dst) in enumerate(
            ((pert_hbm, pert), (probes_hbm, probes), (classes_hbm, classes), (rates_hbm, rates))
        )
    ]
    for load in loads:
        load.start()

    has_up = (row + rows - 1) // rows
    has_down = 1 - (row + 1) // rows
    has_left = (col + cols - 1) // cols
    has_right = 1 - (col + 1) // cols
    has_prev = (me + n - 1) // n
    has_next = 1 - (me + 1) // n
    sides = (
        (has_up, {"row": row - 1}),
        (has_down, {"row": row + 1}),
        (has_left, {"col": col - 1}),
        (has_right, {"col": col + 1}),
        (has_prev, {"member": me - 1}),
        (has_next, {"member": me + 1}),
    )

    barrier = pltpu.get_barrier_semaphore()
    for has, where in sides:
        @pl.when(has == 1)
        def _(where=where):
            pl.semaphore_signal(barrier, inc=1, device_id=where, device_id_type=MESH)

    def remote(src, dst, send, recv, where):
        return pltpu.make_async_remote_copy(
            src_ref=src, dst_ref=dst, send_sem=send, recv_sem=recv,
            device_id=where, device_id_type=MESH,
        )

    for load, which, slot in ((loads[0], pert, me), (loads[1], probes, n)):
        load.wait()
        for pair in range(pairs):
            first = which[2 * pair].astype(F32)
            second = which[2 * pair + 1].astype(F32)
            for part in range(2):
                cut = slice(part * half, (part + 1) * half)
                core[slot, pair, part] = jnp.concatenate([first[cut], second[cut]], 0).astype(jnp.bfloat16)
    lane = lax.broadcasted_iota(jnp.int32, (tile_rows, 128), 1)
    for at, which in enumerate((pert, probes)):
        to_left = jnp.zeros((tile_rows, 128), F32)
        to_right = jnp.zeros((tile_rows, 128), F32)
        for slab in range(slabs):
            low = SWEEPS * slab
            head = which[slab, :, 0:128].astype(F32)
            tail = which[slab, :, tile_cols - 128 : tile_cols].astype(F32)
            if slab:
                head = pltpu.roll(head, low, 1)
                tail = pltpu.roll(tail, 128 - low, 1)
            to_left = jnp.where((lane >= low) & (lane < low + SWEEPS), head, to_left)
            to_right = jnp.where((lane >= 128 - SWEEPS - low) & (lane < 128 - low), tail, to_right)
        side_out[0, at] = to_left.astype(jnp.bfloat16)
        side_out[1, at] = to_right.astype(jnp.bfloat16)
    loads[2].wait()
    loads[3].wait()
    cls[:, 0:tile_cols] = classes[...]

    @pl.when(has_up == 0)
    def _():
        above[...] = jnp.zeros_like(above)
        side_above[...] = jnp.zeros_like(side_above)
        cls_above[...] = jnp.full_like(cls_above, -1)

    @pl.when(has_down == 0)
    def _():
        below[...] = jnp.zeros_like(below)
        side_below[...] = jnp.zeros_like(side_below)
        cls_below[...] = jnp.full_like(cls_below, -1)

    @pl.when(has_right == 0)
    def _():
        side_in[0] = jnp.zeros_like(side_in[0])
        cls_in[0] = jnp.full_like(cls_in[0], -1)

    @pl.when(has_left == 0)
    def _():
        side_in[1] = jnp.zeros_like(side_in[1])
        cls_in[1] = jnp.full_like(cls_in[1], -1)

    pl.semaphore_wait(barrier, has_up + has_down + has_left + has_right + has_prev + has_next)

    def x_copies(at):
        where = sides[2 + at][1]
        block = (0, tile_cols - 128)[at]
        return (
            remote(side_out.at[at], side_in.at[at], x_send.at[at], x_recv.at[at], where),
            remote(classes.at[:, block : block + 128], cls_in.at[at], cx_send.at[at], cx_recv.at[at], where),
        )

    def z_copy(slot, pair, at):
        return remote(
            core.at[slot, pair], core.at[slot, pair],
            z_send.at[slot, pair, at], z_recv.at[slot, pair], sides[4 + at][1],
        )

    def zs_copy(slot, at):
        return remote(
            side.at[slot], side.at[slot], zs_send.at[slot, at], zs_recv.at[slot], sides[4 + at][1]
        )

    def y_copy(slot, pair, at):
        return remote(
            core.at[slot, pair, at], (below, above)[at].at[slot, pair],
            y_send.at[slot, pair, at], y_recv.at[slot, pair, at], sides[at][1],
        )

    def ys_copy(slot, at):
        return remote(
            side.at[slot], (side_below, side_above)[at].at[slot],
            ys_send.at[slot, at], ys_recv.at[slot, at], sides[at][1],
        )

    def cy_copy(at):
        return remote(
            cls.at[at * half : (at + 1) * half], (cls_below, cls_above)[at],
            cy_send.at[at], cy_recv.at[at], sides[at][1],
        )

    def if_sent(at):
        return pl.when(sides[at][0] == 1)

    for at in range(2):
        @if_sent(2 + at)
        def _(at=at):
            for copy in x_copies(at):
                copy.start()

    for pair in range(pairs):
        for at in range(2):
            @if_sent(4 + at)
            def _(pair=pair, at=at):
                z_copy(me, pair, at).start()

    for slot in (n, me):
        for pair in range(pairs):
            for at in range(2):
                @if_sent(at)
                def _(slot=slot, pair=pair, at=at):
                    y_copy(slot, pair, at).start()

    for at in range(2):
        @if_sent(3 - at)
        def _(at=at):
            for copy in x_copies(at):
                copy.wait_recv()

    for at, slot in enumerate((me, n)):
        merged = jnp.where(lane < 64, side_in[0, at].astype(F32), side_in[1, at].astype(F32))
        side[slot] = merged.astype(jnp.bfloat16)
    cls[:, tile_cols:wide] = jnp.where(lane < 64, cls_in[0], cls_in[1])

    for slot in (n, me):
        for at in range(2):
            @if_sent(at)
            def _(slot=slot, at=at):
                ys_copy(slot, at).start()

    for at in range(2):
        @if_sent(at)
        def _(at=at):
            cy_copy(at).start()

    for at in range(2):
        @if_sent(4 + at)
        def _(at=at):
            zs_copy(me, at).start()

    low_rows = lax.broadcasted_iota(jnp.int32, (2 * half, tile_cols), 0) % half < half // 2
    low_side = lax.broadcasted_iota(jnp.int32, (half, 128), 0) < half // 2
    lane_tall = lax.broadcasted_iota(jnp.int32, (tall, 128), 1) < 64

    def widened(slot, pair):
        head = core[slot, pair, 0].astype(F32)
        tail = core[slot, pair, 1].astype(F32)
        rim = jnp.where(low_rows, below[slot, pair].astype(F32), above[slot, pair].astype(F32))
        side_rim = jnp.where(
            low_side,
            side_below[slot].astype(F32)[0:half],
            side_above[slot].astype(F32)[half : 2 * half],
        )
        beside = jnp.concatenate([side[slot].astype(F32), side_rim], 0)
        both = []
        for at in range(2):
            low = SWEEPS * (2 * pair + at)
            cut = slice(at * half, (at + 1) * half)
            mine = jnp.concatenate([head[cut], tail[cut], rim[cut]], 0)
            end = jnp.where(
                lane_tall,
                pltpu.roll(beside, lax.rem(128 - low, 128), 1),
                pltpu.roll(beside, low, 1),
            )
            both.append(jnp.concatenate([mine, end], 1))
        return both

    def y_arrival(slot, pair):
        for at in range(2):
            @if_sent(1 - at)
            def _(at=at):
                y_copy(slot, pair, at).wait_recv()

    def ys_arrival(slot):
        for at in range(2):
            @if_sent(1 - at)
            def _(at=at):
                ys_copy(slot, at).wait_recv()

    for at in range(2):
        @if_sent(1 - at)
        def _(at=at):
            cy_copy(at).wait_recv()

    low_cls = lax.broadcasted_iota(jnp.int32, (half, wide), 0) < half // 2
    kind = jnp.concatenate([cls[...], jnp.where(low_cls, cls_below[...], cls_above[...])], 0)
    picked = jnp.zeros((tall, wide), F32)
    for level in range(rates.shape[0]):
        picked = jnp.where(kind == level, rates[level], picked)
    rate[...] = picked
    keep[...] = 1.0 - 4.0 * picked

    ys_arrival(n)

    @pl.loop(0, pairs)
    def _(pair):
        y_arrival(n, pair)
        for at, field in enumerate(widened(n, pair)):
            probe_field[2 * pair + at] = field * (1.0 / (n - 1))
            out[2 * pair + at] = jnp.zeros((tile_rows, tile_cols), F32)

    def add_pair(slot, pair):
        y_arrival(slot, pair)
        for at, member in enumerate(widened(slot, pair)):
            slab = 2 * pair + at
            field = member * probe_field[slab]
            for _ in range(SWEEPS):
                beside = (
                    pltpu.roll(field, 1, 0) + pltpu.roll(field, tall - 1, 0)
                    + pltpu.roll(field, 1, 1) + pltpu.roll(field, wide - 1, 1)
                )
                field = keep[...] * field + rate[...] * beside
            out[slab] += member[0:tile_rows, 0:tile_cols] * field[0:tile_rows, 0:tile_cols]

    def hand_on(slot, pair, onward):
        z_copy(slot, pair, onward).wait_recv()

        @if_sent(4 + onward)
        def _():
            z_copy(slot, pair, onward).start()

        for at in range(2):
            @if_sent(at)
            def _(at=at):
                y_copy(slot, pair, at).start()

    def hand_on_side(slot, onward):
        zs_copy(slot, onward).wait_recv()

        @if_sent(4 + onward)
        def _():
            zs_copy(slot, onward).start()

        for at in range(2):
            @if_sent(at)
            def _(at=at):
                ys_copy(slot, at).start()

    def at_distance(away, act):
        @pl.when(me - away >= 0)
        def _():
            act(me - away, 1)

        @pl.when(me + away < n)
        def _():
            act(me + away, 0)

    ys_arrival(me)

    @pl.loop(0, pairs)
    def _(pair):
        at_distance(1, lambda slot, onward: hand_on(slot, pair, onward))
        add_pair(me, pair)

    at_distance(1, hand_on_side)

    @pl.loop(1, n)
    def _(away):
        at_distance(away, lambda slot, onward: ys_arrival(slot))

        @pl.loop(0, pairs)
        def _(pair):
            at_distance(away + 1, lambda slot, onward: hand_on(slot, pair, onward))
            at_distance(away, lambda slot, onward: add_pair(slot, pair))

        at_distance(away + 1, hand_on_side)

    @pl.loop(0, n)
    def _(slot):
        for at in range(2):
            @pl.when((sides[4 + at][0] == 1) & ((slot >= me) if at == 0 else (slot <= me)))
            def _(at=at):
                for pair in range(pairs):
                    z_copy(slot, pair, at).wait_send()
                zs_copy(slot, at).wait_send()

    @pl.loop(0, n + 1)
    def _(slot):
        for at in range(2):
            @if_sent(at)
            def _(at=at):
                for pair in range(pairs):
                    y_copy(slot, pair, at).wait_send()
                ys_copy(slot, at).wait_send()

    for at in range(2):
        @if_sent(at)
        def _(at=at):
            cy_copy(at).wait_send()

        @if_sent(2 + at)
        def _(at=at):
            for copy in x_copies(at):
                copy.wait_send()


def body(n, rows, cols, pert, probes, diff_class, class_rate):
    mem_local, variables, levels, tile_rows, tile_cols = pert.shape
    slabs = variables * levels
    pairs = slabs // 2
    half = tile_rows // 2
    wide = tile_cols + 128
    tall = tile_rows + half
    bf16 = jnp.bfloat16
    flat = (slabs, tile_rows, tile_cols)
    vmem = pl.BlockSpec(memory_space=pltpu.VMEM)
    dma = pltpu.SemaphoreType.DMA
    out = pl.pallas_call(
        functools.partial(kernel, n, rows, cols),
        out_shape=jax.ShapeDtypeStruct(flat, F32),
        in_specs=[pl.BlockSpec(memory_space=pltpu.HBM)] * 4,
        out_specs=vmem,
        scratch_shapes=[
            pltpu.VMEM(flat, bf16),
            pltpu.VMEM(flat, bf16),
            pltpu.VMEM((tile_rows, tile_cols), jnp.int32),
            pltpu.SMEM(class_rate.shape, F32),
            pltpu.VMEM((n + 1, pairs, 2, tile_rows, tile_cols), bf16),
            pltpu.VMEM((n + 1, pairs, tile_rows, tile_cols), bf16),
            pltpu.VMEM((n + 1, pairs, tile_rows, tile_cols), bf16),
            pltpu.VMEM((n + 1, tile_rows, 128), bf16),
            pltpu.VMEM((n + 1, tile_rows, 128), bf16),
            pltpu.VMEM((n + 1, tile_rows, 128), bf16),
            pltpu.VMEM((2, 2, tile_rows, 128), bf16),
            pltpu.VMEM((2, 2, tile_rows, 128), bf16),
            pltpu.VMEM((tile_rows, wide), jnp.int32),
            pltpu.VMEM((2, tile_rows, 128), jnp.int32),
            pltpu.VMEM((half, wide), jnp.int32),
            pltpu.VMEM((half, wide), jnp.int32),
            pltpu.VMEM((slabs, tall, wide), F32),
            pltpu.VMEM((tall, wide), F32),
            pltpu.VMEM((tall, wide), F32),
            dma((4,)), dma((n, pairs, 2)), dma((n, pairs)), dma((n, 2)), dma((n,)),
            dma((n + 1, pairs, 2)), dma((n + 1, pairs, 2)), dma((n + 1, 2)), dma((n + 1, 2)),
            dma((2,)), dma((2,)), dma((2,)), dma((2,)), dma((2,)), dma((2,)),
        ],
        compiler_params=pltpu.CompilerParams(
            collective_id=0, has_side_effects=True, vmem_limit_bytes=64 * 1024 * 1024
        ),
    )(pert.reshape(flat), probes.reshape(flat), diff_class, class_rate)
    return out.reshape(pert.shape)


def solution(mesh):
    placed = (
        P("member", None, None, "row", "col"),
        P("member", None, None, "row", "col"),
        P("row", "col"),
        P(),
    )
    sizes = (mesh.shape["member"], mesh.shape["row"], mesh.shape["col"])
    return jax.shard_map(
        functools.partial(body, *sizes),
        mesh=mesh,
        in_specs=placed,
        out_specs=P("member", None, None, "row", "col"),
        check_vma=False,
    )
```

```python
import functools

import jax
import jax.numpy as jnp
from jax import lax
from jax.experimental import pallas as pl
from jax.experimental.pallas import tpu as pltpu
from jax.sharding import PartitionSpec as P

SWEEPS = 4
SUBLANES = 8
MESH = pl.DeviceIdType.MESH
F32 = jnp.float32


def kernel(
    n, rows, cols,
    pert_hbm, probes_hbm, classes_hbm, rates_hbm, out,
    pert, probes, classes, rates,
    core, above, below, side, side_above, side_below,
    side_out, side_in, cls, cls_in, cls_above, cls_below,
    probe_field, keep, rate, turned, field_a, field_b, result,
    in_sem, z_send, z_recv, zs_send, zs_recv, y_send, y_recv, ys_send, ys_recv,
    x_send, x_recv, cx_send, cx_recv, cy_send, cy_recv,
):
    slabs, tile_rows, tile_cols = pert.shape
    pairs = slabs // 2
    half = tile_rows // 2
    wide = tile_cols + 128
    tall = tile_rows + half
    me = lax.axis_index("member")
    row = lax.axis_index("row")
    col = lax.axis_index("col")

    loads = [
        pltpu.make_async_copy(src, dst, in_sem.at[at])
        for at, (src, dst) in enumerate(
            ((pert_hbm, pert), (probes_hbm, probes), (classes_hbm, classes), (rates_hbm, rates))
        )
    ]
    for load in loads:
        load.start()

    has_up = (row + rows - 1) // rows
    has_down = 1 - (row + 1) // rows
    has_left = (col + cols - 1) // cols
    has_right = 1 - (col + 1) // cols
    has_prev = (me + n - 1) // n
    has_next = 1 - (me + 1) // n
    sides = (
        (has_up, {"row": row - 1}),
        (has_down, {"row": row + 1}),
        (has_left, {"col": col - 1}),
        (has_right, {"col": col + 1}),
        (has_prev, {"member": me - 1}),
        (has_next, {"member": me + 1}),
    )

    barrier = pltpu.get_barrier_semaphore()
    for has, where in sides:
        @pl.when(has == 1)
        def _(where=where):
            pl.semaphore_signal(barrier, inc=1, device_id=where, device_id_type=MESH)

    def remote(src, dst, send, recv, where):
        return pltpu.make_async_remote_copy(
            src_ref=src, dst_ref=dst, send_sem=send, recv_sem=recv,
            device_id=where, device_id_type=MESH,
        )

    for load, which, slot in ((loads[0], pert, me), (loads[1], probes, n)):
        load.wait()
        for pair in range(pairs):
            first = which[2 * pair].astype(F32)
            second = which[2 * pair + 1].astype(F32)
            for part in range(2):
                cut = slice(part * half, (part + 1) * half)
                core[slot, pair, part] = jnp.concatenate([first[cut], second[cut]], 0).astype(jnp.bfloat16)
    lane = lax.broadcasted_iota(jnp.int32, (tile_rows, 128), 1)
    for at, which in enumerate((pert, probes)):
        to_left = jnp.zeros((tile_rows, 128), F32)
        to_right = jnp.zeros((tile_rows, 128), F32)
        for slab in range(slabs):
            low = SWEEPS * slab
            head = which[slab, :, 0:128].astype(F32)
            tail = which[slab, :, tile_cols - 128 : tile_cols].astype(F32)
            if slab:
                head = pltpu.roll(head, low, 1)
                tail = pltpu.roll(tail, 128 - low, 1)
            to_left = jnp.where((lane >= low) & (lane < low + SWEEPS), head, to_left)
            to_right = jnp.where((lane >= 128 - SWEEPS - low) & (lane < 128 - low), tail, to_right)
        side_out[0, at] = to_left.astype(jnp.bfloat16)
        side_out[1, at] = to_right.astype(jnp.bfloat16)
    loads[2].wait()
    loads[3].wait()
    cls[:, 0:tile_cols] = classes[...]

    @pl.when(has_up == 0)
    def _():
        above[...] = jnp.zeros_like(above)
        side_above[...] = jnp.zeros_like(side_above)
        cls_above[...] = jnp.full_like(cls_above, -1)

    @pl.when(has_down == 0)
    def _():
        below[...] = jnp.zeros_like(below)
        side_below[...] = jnp.zeros_like(side_below)
        cls_below[...] = jnp.full_like(cls_below, -1)

    @pl.when(has_right == 0)
    def _():
        side_in[0] = jnp.zeros_like(side_in[0])
        cls_in[0] = jnp.full_like(cls_in[0], -1)

    @pl.when(has_left == 0)
    def _():
        side_in[1] = jnp.zeros_like(side_in[1])
        cls_in[1] = jnp.full_like(cls_in[1], -1)

    pl.semaphore_wait(barrier, has_up + has_down + has_left + has_right + has_prev + has_next)

    def x_copies(at):
        where = sides[2 + at][1]
        block = (0, tile_cols - 128)[at]
        return (
            remote(side_out.at[at], side_in.at[at], x_send.at[at], x_recv.at[at], where),
            remote(classes.at[:, block : block + 128], cls_in.at[at], cx_send.at[at], cx_recv.at[at], where),
        )

    def z_copy(slot, pair, at):
        return remote(
            core.at[slot, pair], core.at[slot, pair],
            z_send.at[slot, pair, at], z_recv.at[slot, pair], sides[4 + at][1],
        )

    def zs_copy(slot, at):
        return remote(
            side.at[slot], side.at[slot], zs_send.at[slot, at], zs_recv.at[slot], sides[4 + at][1]
        )

    def y_copy(slot, pair, at):
        return remote(
            core.at[slot, pair, at], (below, above)[at].at[slot, pair],
            y_send.at[slot, pair, at], y_recv.at[slot, pair, at], sides[at][1],
        )

    def ys_copy(slot, at):
        return remote(
            side.at[slot], (side_below, side_above)[at].at[slot],
            ys_send.at[slot, at], ys_recv.at[slot, at], sides[at][1],
        )

    def cy_copy(at):
        return remote(
            cls.at[at * half : (at + 1) * half], (cls_below, cls_above)[at],
            cy_send.at[at], cy_recv.at[at], sides[at][1],
        )

    def if_sent(at):
        return pl.when(sides[at][0] == 1)

    for at in range(2):
        @if_sent(2 + at)
        def _(at=at):
            for copy in x_copies(at):
                copy.start()

    for pair in range(pairs):
        for at in range(2):
            @if_sent(4 + at)
            def _(pair=pair, at=at):
                z_copy(me, pair, at).start()

    for slot in (n, me):
        for pair in range(pairs):
            for at in range(2):
                @if_sent(at)
                def _(slot=slot, pair=pair, at=at):
                    y_copy(slot, pair, at).start()

    for at in range(2):
        @if_sent(3 - at)
        def _(at=at):
            for copy in x_copies(at):
                copy.wait_recv()

    for at, slot in enumerate((me, n)):
        merged = jnp.where(lane < 64, side_in[0, at].astype(F32), side_in[1, at].astype(F32))
        side[slot] = merged.astype(jnp.bfloat16)
    cls[:, tile_cols:wide] = jnp.where(lane < 64, cls_in[0], cls_in[1])

    for slot in (n, me):
        for at in range(2):
            @if_sent(at)
            def _(slot=slot, at=at):
                ys_copy(slot, at).start()

    for at in range(2):
        @if_sent(at)
        def _(at=at):
            cy_copy(at).start()

    for at in range(2):
        @if_sent(4 + at)
        def _(at=at):
            zs_copy(me, at).start()

    low_rows = lax.broadcasted_iota(jnp.int32, (2 * half, tile_cols), 0) % half < half // 2
    low_side = lax.broadcasted_iota(jnp.int32, (half, 128), 0) < half // 2
    lane_tall = lax.broadcasted_iota(jnp.int32, (tall, 128), 1) < 64

    def widened(slot, pair):
        head = core[slot, pair, 0].astype(F32)
        tail = core[slot, pair, 1].astype(F32)
        rim = jnp.where(low_rows, below[slot, pair].astype(F32), above[slot, pair].astype(F32))
        side_rim = jnp.where(
            low_side,
            side_below[slot].astype(F32)[0:half],
            side_above[slot].astype(F32)[half : 2 * half],
        )
        beside = jnp.concatenate([side[slot].astype(F32), side_rim], 0)
        both = []
        for at in range(2):
            low = SWEEPS * (2 * pair + at)
            cut = slice(at * half, (at + 1) * half)
            mine = jnp.concatenate([head[cut], tail[cut], rim[cut]], 0)
            end = jnp.where(
                lane_tall,
                pltpu.roll(beside, lax.rem(128 - low, 128), 1),
                pltpu.roll(beside, low, 1),
            )
            both.append(jnp.concatenate([mine, end], 1))
        return both

    def y_arrival(slot, pair):
        for at in range(2):
            @if_sent(1 - at)
            def _(at=at):
                y_copy(slot, pair, at).wait_recv()

    def ys_arrival(slot):
        for at in range(2):
            @if_sent(1 - at)
            def _(at=at):
                ys_copy(slot, at).wait_recv()

    for at in range(2):
        @if_sent(1 - at)
        def _(at=at):
            cy_copy(at).wait_recv()

    low_cls = lax.broadcasted_iota(jnp.int32, (half, wide), 0) < half // 2
    kind = jnp.concatenate([cls[...], jnp.where(low_cls, cls_below[...], cls_above[...])], 0)
    picked = jnp.zeros((tall, wide), F32)
    for level in range(rates.shape[0]):
        picked = jnp.where(kind == level, rates[level], picked)
    for at in range(tall):
        line = jnp.broadcast_to(picked[at : at + 1], (SUBLANES, wide))
        rate[at] = line
        keep[at] = 1.0 - 4.0 * line

    ys_arrival(n)

    @pl.loop(0, pairs)
    def _(pair):
        y_arrival(n, pair)
        for at, field in enumerate(widened(n, pair)):
            probe_field[2 * pair + at] = field
            out[2 * pair + at] = jnp.zeros((tile_rows, tile_cols), F32)

    blocks = wide // 128
    if slabs < SUBLANES:
        turned[:, slabs * tall :] = jnp.zeros((blocks, (SUBLANES - slabs) * tall, 128), F32)

    def sweep(load, store, margin):
        above_now, now = load(-margin - 1), load(-margin)
        for at in range(-margin, tile_rows + margin):
            below_now = load(at + 1)
            beside = above_now + below_now + pltpu.roll(now, 1, 1) + pltpu.roll(now, wide - 1, 1)
            store(at, keep[at % tall] * now + rate[at % tall] * beside)
            above_now, now = now, below_now

    def load_turned(at):
        picks = [
            turned[block, pl.ds(at % tall, SUBLANES, stride=tall), :] for block in range(blocks)
        ]
        return jnp.concatenate(picks, 1)

    def store_result(at, value):
        for block in range(tile_cols // 128):
            result[block, pl.ds(at, SUBLANES, stride=tile_rows), :] = value[:, block * 128 : (block + 1) * 128]

    def through(buffer):
        def load(at):
            return buffer[at % tall]

        def store(at, value):
            buffer[at % tall] = value

        return load, store

    def add_member(slot):
        for pair in range(pairs):
            y_arrival(slot, pair)
        ys_arrival(slot)
        for pair in range(pairs):
            for at, member in enumerate(widened(slot, pair)):
                slab = 2 * pair + at
                field = member * probe_field[slab]
                for block in range(blocks):
                    turned[block, slab * tall : (slab + 1) * tall] = field[:, block * 128 : (block + 1) * 128]
        load_a, store_a = through(field_a)
        load_b, store_b = through(field_b)
        loads_now = load_turned
        for step in range(SWEEPS):
            store_now = store_result if step == SWEEPS - 1 else (store_a, store_b)[step % 2]
            sweep(loads_now, store_now, SWEEPS - 1 - step)
            loads_now = (load_a, load_b)[step % 2]
        for pair in range(pairs):
            head = core[slot, pair, 0].astype(F32)
            tail = core[slot, pair, 1].astype(F32)
            for at in range(2):
                slab = 2 * pair + at
                cut = slice(at * half, (at + 1) * half)
                member = jnp.concatenate([head[cut], tail[cut]], 0)
                done = jnp.concatenate(
                    [result[block, slab * tile_rows : (slab + 1) * tile_rows] for block in range(tile_cols // 128)], 1
                )
                out[slab] += member * done

    def hand_on(slot, pair, onward):
        z_copy(slot, pair, onward).wait_recv()

        @if_sent(4 + onward)
        def _():
            z_copy(slot, pair, onward).start()

        for at in range(2):
            @if_sent(at)
            def _(at=at):
                y_copy(slot, pair, at).start()

    def hand_on_side(slot, onward):
        zs_copy(slot, onward).wait_recv()

        @if_sent(4 + onward)
        def _():
            zs_copy(slot, onward).start()

        for at in range(2):
            @if_sent(at)
            def _(at=at):
                ys_copy(slot, at).start()

    def at_distance(away, act):
        @pl.when(me - away >= 0)
        def _():
            act(me - away, 1)

        @pl.when(me + away < n)
        def _():
            act(me + away, 0)

    def around(away, work):
        early = pairs - 1
        for pair in range(early):
            at_distance(away, lambda slot, onward: hand_on(slot, pair, onward))
        work()
        at_distance(away, lambda slot, onward: hand_on(slot, early, onward))
        at_distance(away, hand_on_side)

    around(1, lambda: add_member(me))

    @pl.loop(1, n)
    def _(away):
        around(away + 1, lambda: at_distance(away, lambda slot, onward: add_member(slot)))

    @pl.loop(0, n)
    def _(slot):
        for at in range(2):
            @pl.when((sides[4 + at][0] == 1) & ((slot >= me) if at == 0 else (slot <= me)))
            def _(at=at):
                for pair in range(pairs):
                    z_copy(slot, pair, at).wait_send()
                zs_copy(slot, at).wait_send()

    @pl.loop(0, n + 1)
    def _(slot):
        for at in range(2):
            @if_sent(at)
            def _(at=at):
                for pair in range(pairs):
                    y_copy(slot, pair, at).wait_send()
                ys_copy(slot, at).wait_send()

    for at in range(2):
        @if_sent(at)
        def _(at=at):
            cy_copy(at).wait_send()

        @if_sent(2 + at)
        def _(at=at):
            for copy in x_copies(at):
                copy.wait_send()


def body(n, rows, cols, pert, probes, diff_class, class_rate):
    mem_local, variables, levels, tile_rows, tile_cols = pert.shape
    slabs = variables * levels
    pairs = slabs // 2
    half = tile_rows // 2
    wide = tile_cols + 128
    tall = tile_rows + half
    bf16 = jnp.bfloat16
    flat = (slabs, tile_rows, tile_cols)
    vmem = pl.BlockSpec(memory_space=pltpu.VMEM)
    dma = pltpu.SemaphoreType.DMA
    out = pl.pallas_call(
        functools.partial(kernel, n, rows, cols),
        out_shape=jax.ShapeDtypeStruct(flat, F32),
        in_specs=[pl.BlockSpec(memory_space=pltpu.HBM)] * 4,
        out_specs=vmem,
        scratch_shapes=[
            pltpu.VMEM(flat, bf16),
            pltpu.VMEM(flat, bf16),
            pltpu.VMEM((tile_rows, tile_cols), jnp.int32),
            pltpu.SMEM(class_rate.shape, F32),
            pltpu.VMEM((n + 1, pairs, 2, tile_rows, tile_cols), bf16),
            pltpu.VMEM((n + 1, pairs, tile_rows, tile_cols), bf16),
            pltpu.VMEM((n + 1, pairs, tile_rows, tile_cols), bf16),
            pltpu.VMEM((n + 1, tile_rows, 128), bf16),
            pltpu.VMEM((n + 1, tile_rows, 128), bf16),
            pltpu.VMEM((n + 1, tile_rows, 128), bf16),
            pltpu.VMEM((2, 2, tile_rows, 128), bf16),
            pltpu.VMEM((2, 2, tile_rows, 128), bf16),
            pltpu.VMEM((tile_rows, wide), jnp.int32),
            pltpu.VMEM((2, tile_rows, 128), jnp.int32),
            pltpu.VMEM((half, wide), jnp.int32),
            pltpu.VMEM((half, wide), jnp.int32),
            pltpu.VMEM((slabs, tall, wide), F32),
            pltpu.VMEM((tall, SUBLANES, wide), F32),
            pltpu.VMEM((tall, SUBLANES, wide), F32),
            pltpu.VMEM((wide // 128, SUBLANES * tall, 128), F32),
            pltpu.VMEM((tall, SUBLANES, wide), F32),
            pltpu.VMEM((tall, SUBLANES, wide), F32),
            pltpu.VMEM((tile_cols // 128, SUBLANES * tile_rows, 128), F32),
            dma((4,)), dma((n, pairs, 2)), dma((n, pairs)), dma((n, 2)), dma((n,)),
            dma((n + 1, pairs, 2)), dma((n + 1, pairs, 2)), dma((n + 1, 2)), dma((n + 1, 2)),
            dma((2,)), dma((2,)), dma((2,)), dma((2,)), dma((2,)), dma((2,)),
        ],
        compiler_params=pltpu.CompilerParams(
            collective_id=0, has_side_effects=True, vmem_limit_bytes=64 * 1024 * 1024
        ),
    )(pert.reshape(flat), probes.reshape(flat), diff_class, class_rate)
    return out.reshape(pert.shape) / (n - 1)


def solution(mesh):
    placed = (
        P("member", None, None, "row", "col"),
        P("member", None, None, "row", "col"),
        P("row", "col"),
        P(),
    )
    sizes = (mesh.shape["member"], mesh.shape["row"], mesh.shape["col"])
    return jax.shard_map(
        functools.partial(body, *sizes),
        mesh=mesh,
        in_specs=placed,
        out_specs=P("member", None, None, "row", "col"),
        check_vma=False,
    )
```

```python
import functools

import jax
import jax.numpy as jnp
from jax import lax
from jax.experimental import pallas as pl
from jax.experimental.pallas import tpu as pltpu
from jax.sharding import PartitionSpec as P

SWEEPS = 4
SUBLANES = 8
MESH = pl.DeviceIdType.MESH
F32 = jnp.float32


def kernel(
    n, rows, cols,
    pert_hbm, probes_hbm, classes_hbm, rates_hbm, out,
    pert, probes, classes, rates,
    core, above, below, side, side_above, side_below,
    side_out, side_in, cls, cls_in, cls_above, cls_below,
    probe_field, keep, rate, turned, field_a, field_b, result,
    in_sem, z_send, z_recv, zs_send, zs_recv, y_send, y_recv, ys_send, ys_recv,
    x_send, x_recv, cx_send, cx_recv, cy_send, cy_recv,
):
    slabs, tile_rows, tile_cols = pert.shape
    pairs = slabs // 2
    half = tile_rows // 2
    wide = tile_cols + 128
    tall = tile_rows + half
    me = lax.axis_index("member")
    row = lax.axis_index("row")
    col = lax.axis_index("col")

    loads = [
        pltpu.make_async_copy(src, dst, in_sem.at[at])
        for at, (src, dst) in enumerate(
            ((pert_hbm, pert), (probes_hbm, probes), (classes_hbm, classes), (rates_hbm, rates))
        )
    ]
    for load in loads:
        load.start()

    has_up = (row + rows - 1) // rows
    has_down = 1 - (row + 1) // rows
    has_left = (col + cols - 1) // cols
    has_right = 1 - (col + 1) // cols
    has_prev = (me + n - 1) // n
    has_next = 1 - (me + 1) // n
    sides = (
        (has_up, {"row": row - 1}),
        (has_down, {"row": row + 1}),
        (has_left, {"col": col - 1}),
        (has_right, {"col": col + 1}),
        (has_prev, {"member": me - 1}),
        (has_next, {"member": me + 1}),
    )

    barrier = pltpu.get_barrier_semaphore()
    for has, where in sides:
        @pl.when(has == 1)
        def _(where=where):
            pl.semaphore_signal(barrier, inc=1, device_id=where, device_id_type=MESH)

    def remote(src, dst, send, recv, where):
        return pltpu.make_async_remote_copy(
            src_ref=src, dst_ref=dst, send_sem=send, recv_sem=recv,
            device_id=where, device_id_type=MESH,
        )

    def x_copies(at):
        where = sides[2 + at][1]
        block = (0, tile_cols - 128)[at]
        return (
            remote(side_out.at[at], side_in.at[at], x_send.at[at], x_recv.at[at], where),
            remote(classes.at[:, block : block + 128], cls_in.at[at], cx_send.at[at], cx_recv.at[at], where),
        )

    def z_copy(slot, pair, at):
        return remote(
            core.at[slot, pair], core.at[slot, pair],
            z_send.at[slot, pair, at], z_recv.at[slot, pair], sides[4 + at][1],
        )

    def zs_copy(slot, at):
        return remote(
            side.at[slot], side.at[slot], zs_send.at[slot, at], zs_recv.at[slot], sides[4 + at][1]
        )

    def y_copy(slot, pair, at):
        return remote(
            core.at[slot, pair, at], (below, above)[at].at[slot, pair],
            y_send.at[slot, pair, at], y_recv.at[slot, pair, at], sides[at][1],
        )

    def ys_copy(slot, at):
        return remote(
            side.at[slot], (side_below, side_above)[at].at[slot],
            ys_send.at[slot, at], ys_recv.at[slot, at], sides[at][1],
        )

    def cy_copy(at):
        return remote(
            cls.at[at * half : (at + 1) * half], (cls_below, cls_above)[at],
            cy_send.at[at], cy_recv.at[at], sides[at][1],
        )

    def if_sent(at):
        return pl.when(sides[at][0] == 1)

    def pack(which, slot):
        for pair in range(pairs):
            first = which[2 * pair].astype(F32)
            second = which[2 * pair + 1].astype(F32)
            for part in range(2):
                cut = slice(part * half, (part + 1) * half)
                core[slot, pair, part] = jnp.concatenate([first[cut], second[cut]], 0).astype(jnp.bfloat16)

    def start_rows(slot):
        for pair in range(pairs):
            for at in range(2):
                @if_sent(at)
                def _(pair=pair, at=at):
                    y_copy(slot, pair, at).start()

    loads[0].wait()
    pack(pert, me)
    pl.semaphore_wait(barrier, has_up + has_down + has_left + has_right + has_prev + has_next)

    for pair in range(pairs):
        for at in range(2):
            @if_sent(4 + at)
            def _(pair=pair, at=at):
                z_copy(me, pair, at).start()

    for load in loads[1:]:
        load.wait()
    lane = lax.broadcasted_iota(jnp.int32, (tile_rows, 128), 1)
    for at, which in enumerate((pert, probes)):
        to_left = jnp.zeros((tile_rows, 128), F32)
        to_right = jnp.zeros((tile_rows, 128), F32)
        for slab in range(slabs):
            low = SWEEPS * slab
            head = which[slab, :, 0:128].astype(F32)
            tail = which[slab, :, tile_cols - 128 : tile_cols].astype(F32)
            if slab:
                head = pltpu.roll(head, low, 1)
                tail = pltpu.roll(tail, 128 - low, 1)
            to_left = jnp.where((lane >= low) & (lane < low + SWEEPS), head, to_left)
            to_right = jnp.where((lane >= 128 - SWEEPS - low) & (lane < 128 - low), tail, to_right)
        side_out[0, at] = to_left.astype(jnp.bfloat16)
        side_out[1, at] = to_right.astype(jnp.bfloat16)
    for at in range(2):
        @if_sent(2 + at)
        def _(at=at):
            for copy in x_copies(at):
                copy.start()

    pack(probes, n)
    start_rows(n)
    start_rows(me)
    cls[:, 0:tile_cols] = classes[...]

    @pl.when(has_up == 0)
    def _():
        above[...] = jnp.zeros_like(above)
        side_above[...] = jnp.zeros_like(side_above)
        cls_above[...] = jnp.full_like(cls_above, -1)

    @pl.when(has_down == 0)
    def _():
        below[...] = jnp.zeros_like(below)
        side_below[...] = jnp.zeros_like(side_below)
        cls_below[...] = jnp.full_like(cls_below, -1)

    @pl.when(has_right == 0)
    def _():
        side_in[0] = jnp.zeros_like(side_in[0])
        cls_in[0] = jnp.full_like(cls_in[0], -1)

    @pl.when(has_left == 0)
    def _():
        side_in[1] = jnp.zeros_like(side_in[1])
        cls_in[1] = jnp.full_like(cls_in[1], -1)

    for at in range(2):
        @if_sent(3 - at)
        def _(at=at):
            for copy in x_copies(at):
                copy.wait_recv()

    for at, slot in enumerate((me, n)):
        merged = jnp.where(lane < 64, side_in[0, at].astype(F32), side_in[1, at].astype(F32))
        side[slot] = merged.astype(jnp.bfloat16)
    cls[:, tile_cols:wide] = jnp.where(lane < 64, cls_in[0], cls_in[1])

    for slot in (n, me):
        for at in range(2):
            @if_sent(at)
            def _(slot=slot, at=at):
                ys_copy(slot, at).start()

    for at in range(2):
        @if_sent(at)
        def _(at=at):
            cy_copy(at).start()

    for at in range(2):
        @if_sent(4 + at)
        def _(at=at):
            zs_copy(me, at).start()

    low_rows = lax.broadcasted_iota(jnp.int32, (2 * half, tile_cols), 0) % half < half // 2
    low_side = lax.broadcasted_iota(jnp.int32, (half, 128), 0) < half // 2
    lane_tall = lax.broadcasted_iota(jnp.int32, (tall, 128), 1) < 64

    def widened(slot, pair):
        head = core[slot, pair, 0].astype(F32)
        tail = core[slot, pair, 1].astype(F32)
        rim = jnp.where(low_rows, below[slot, pair].astype(F32), above[slot, pair].astype(F32))
        side_rim = jnp.where(
            low_side,
            side_below[slot].astype(F32)[0:half],
            side_above[slot].astype(F32)[half : 2 * half],
        )
        beside = jnp.concatenate([side[slot].astype(F32), side_rim], 0)
        both = []
        for at in range(2):
            low = SWEEPS * (2 * pair + at)
            cut = slice(at * half, (at + 1) * half)
            mine = jnp.concatenate([head[cut], tail[cut], rim[cut]], 0)
            end = jnp.where(
                lane_tall,
                pltpu.roll(beside, lax.rem(128 - low, 128), 1),
                pltpu.roll(beside, low, 1),
            )
            both.append(jnp.concatenate([mine, end], 1))
        return both

    def y_arrival(slot, pair):
        for at in range(2):
            @if_sent(1 - at)
            def _(at=at):
                y_copy(slot, pair, at).wait_recv()

    def ys_arrival(slot):
        for at in range(2):
            @if_sent(1 - at)
            def _(at=at):
                ys_copy(slot, at).wait_recv()

    for at in range(2):
        @if_sent(1 - at)
        def _(at=at):
            cy_copy(at).wait_recv()

    low_cls = lax.broadcasted_iota(jnp.int32, (half, wide), 0) < half // 2
    kind = jnp.concatenate([cls[...], jnp.where(low_cls, cls_below[...], cls_above[...])], 0)
    picked = jnp.zeros((tall, wide), F32)
    for level in range(rates.shape[0]):
        picked = jnp.where(kind == level, rates[level], picked)
    for at in range(tall):
        line = jnp.broadcast_to(picked[at : at + 1], (SUBLANES, wide))
        rate[at] = line
        keep[at] = 1.0 - 4.0 * line

    ys_arrival(n)

    @pl.loop(0, pairs)
    def _(pair):
        y_arrival(n, pair)
        for at, field in enumerate(widened(n, pair)):
            probe_field[2 * pair + at] = field
            out[2 * pair + at] = jnp.zeros((tile_rows, tile_cols), F32)

    blocks = wide // 128
    if slabs < SUBLANES:
        turned[:, slabs * tall :] = jnp.zeros((blocks, (SUBLANES - slabs) * tall, 128), F32)

    def sweep(load, store, margin):
        above_now, now = load(-margin - 1), load(-margin)
        for at in range(-margin, tile_rows + margin):
            below_now = load(at + 1)
            beside = above_now + below_now + pltpu.roll(now, 1, 1) + pltpu.roll(now, wide - 1, 1)
            store(at, keep[at % tall] * now + rate[at % tall] * beside)
            above_now, now = now, below_now

    def load_turned(at):
        picks = [
            turned[block, pl.ds(at % tall, SUBLANES, stride=tall), :] for block in range(blocks)
        ]
        return jnp.concatenate(picks, 1)

    def store_result(at, value):
        for block in range(tile_cols // 128):
            result[block, pl.ds(at, SUBLANES, stride=tile_rows), :] = value[:, block * 128 : (block + 1) * 128]

    def through(buffer):
        def load(at):
            return buffer[at % tall]

        def store(at, value):
            buffer[at % tall] = value

        return load, store

    def add_member(slot):
        for pair in range(pairs):
            y_arrival(slot, pair)
        ys_arrival(slot)
        for pair in range(pairs):
            for at, member in enumerate(widened(slot, pair)):
                slab = 2 * pair + at
                field = member * probe_field[slab]
                for block in range(blocks):
                    turned[block, slab * tall : (slab + 1) * tall] = field[:, block * 128 : (block + 1) * 128]
        load_a, store_a = through(field_a)
        load_b, store_b = through(field_b)
        loads_now = load_turned
        for step in range(SWEEPS):
            store_now = store_result if step == SWEEPS - 1 else (store_a, store_b)[step % 2]
            sweep(loads_now, store_now, SWEEPS - 1 - step)
            loads_now = (load_a, load_b)[step % 2]
        for pair in range(pairs):
            head = core[slot, pair, 0].astype(F32)
            tail = core[slot, pair, 1].astype(F32)
            for at in range(2):
                slab = 2 * pair + at
                cut = slice(at * half, (at + 1) * half)
                member = jnp.concatenate([head[cut], tail[cut]], 0)
                done = jnp.concatenate(
                    [result[block, slab * tile_rows : (slab + 1) * tile_rows] for block in range(tile_cols // 128)], 1
                )
                out[slab] += member * done

    def hand_on(slot, pair, onward):
        z_copy(slot, pair, onward).wait_recv()

        @if_sent(4 + onward)
        def _():
            z_copy(slot, pair, onward).start()

        for at in range(2):
            @if_sent(at)
            def _(at=at):
                y_copy(slot, pair, at).start()

    def hand_on_side(slot, onward):
        zs_copy(slot, onward).wait_recv()

        @if_sent(4 + onward)
        def _():
            zs_copy(slot, onward).start()

        for at in range(2):
            @if_sent(at)
            def _(at=at):
                ys_copy(slot, at).start()

    def at_distance(away, act):
        @pl.when(me - away >= 0)
        def _():
            act(me - away, 1)

        @pl.when(me + away < n)
        def _():
            act(me + away, 0)

    def arrivals(away):
        for pair in range(pairs):
            at_distance(away, lambda slot, onward: hand_on(slot, pair, onward))
        at_distance(away, hand_on_side)

    lower = 1 - (2 * me) // n

    @pl.loop(0, 2 * n)
    def _(turn):
        away = turn // 2
        second = turn % 2
        slot = me + away * (2 * ((second + lower) % 2) - 1)

        @pl.when(second == 1)
        def _():
            arrivals(away + 1)

        @pl.when((slot >= 0) & (slot < n) & (turn > 0))
        def _():
            add_member(slot)

    @pl.loop(0, n)
    def _(slot):
        for at in range(2):
            @pl.when((sides[4 + at][0] == 1) & ((slot >= me) if at == 0 else (slot <= me)))
            def _(at=at):
                for pair in range(pairs):
                    z_copy(slot, pair, at).wait_send()
                zs_copy(slot, at).wait_send()

    @pl.loop(0, n + 1)
    def _(slot):
        for at in range(2):
            @if_sent(at)
            def _(at=at):
                for pair in range(pairs):
                    y_copy(slot, pair, at).wait_send()
                ys_copy(slot, at).wait_send()

    for at in range(2):
        @if_sent(at)
        def _(at=at):
            cy_copy(at).wait_send()

        @if_sent(2 + at)
        def _(at=at):
            for copy in x_copies(at):
                copy.wait_send()


def body(n, rows, cols, pert, probes, diff_class, class_rate):
    mem_local, variables, levels, tile_rows, tile_cols = pert.shape
    slabs = variables * levels
    pairs = slabs // 2
    half = tile_rows // 2
    wide = tile_cols + 128
    tall = tile_rows + half
    bf16 = jnp.bfloat16
    flat = (slabs, tile_rows, tile_cols)
    vmem = pl.BlockSpec(memory_space=pltpu.VMEM)
    dma = pltpu.SemaphoreType.DMA
    out = pl.pallas_call(
        functools.partial(kernel, n, rows, cols),
        out_shape=pltpu.VMEM(flat, F32),
        in_specs=[pl.BlockSpec(memory_space=pltpu.HBM)] * 4,
        out_specs=vmem,
        scratch_shapes=[
            pltpu.VMEM(flat, bf16),
            pltpu.VMEM(flat, bf16),
            pltpu.VMEM((tile_rows, tile_cols), jnp.int32),
            pltpu.SMEM(class_rate.shape, F32),
            pltpu.VMEM((n + 1, pairs, 2, tile_rows, tile_cols), bf16),
            pltpu.VMEM((n + 1, pairs, tile_rows, tile_cols), bf16),
            pltpu.VMEM((n + 1, pairs, tile_rows, tile_cols), bf16),
            pltpu.VMEM((n + 1, tile_rows, 128), bf16),
            pltpu.VMEM((n + 1, tile_rows, 128), bf16),
            pltpu.VMEM((n + 1, tile_rows, 128), bf16),
            pltpu.VMEM((2, 2, tile_rows, 128), bf16),
            pltpu.VMEM((2, 2, tile_rows, 128), bf16),
            pltpu.VMEM((tile_rows, wide), jnp.int32),
            pltpu.VMEM((2, tile_rows, 128), jnp.int32),
            pltpu.VMEM((half, wide), jnp.int32),
            pltpu.VMEM((half, wide), jnp.int32),
            pltpu.VMEM((slabs, tall, wide), F32),
            pltpu.VMEM((tall, SUBLANES, wide), F32),
            pltpu.VMEM((tall, SUBLANES, wide), F32),
            pltpu.VMEM((wide // 128, SUBLANES * tall, 128), F32),
            pltpu.VMEM((tall, SUBLANES, wide), F32),
            pltpu.VMEM((tall, SUBLANES, wide), F32),
            pltpu.VMEM((tile_cols // 128, SUBLANES * tile_rows, 128), F32),
            dma((4,)), dma((n, pairs, 2)), dma((n, pairs)), dma((n, 2)), dma((n,)),
            dma((n + 1, pairs, 2)), dma((n + 1, pairs, 2)), dma((n + 1, 2)), dma((n + 1, 2)),
            dma((2,)), dma((2,)), dma((2,)), dma((2,)), dma((2,)), dma((2,)),
        ],
        compiler_params=pltpu.CompilerParams(
            collective_id=0, has_side_effects=True, vmem_limit_bytes=60 * 1024 * 1024
        ),
    )(pert.reshape(flat), probes.reshape(flat), diff_class, class_rate)
    return out.reshape(pert.shape) / (n - 1)


def solution(mesh):
    placed = (
        P("member", None, None, "row", "col"),
        P("member", None, None, "row", "col"),
        P("row", "col"),
        P(),
    )
    sizes = (mesh.shape["member"], mesh.shape["row"], mesh.shape["col"])
    return jax.shard_map(
        functools.partial(body, *sizes),
        mesh=mesh,
        in_specs=placed,
        out_specs=P("member", None, None, "row", "col"),
        check_vma=False,
    )
```

```python
import functools

import jax
import jax.numpy as jnp
from jax import lax
from jax.experimental import pallas as pl
from jax.experimental.pallas import tpu as pltpu
from jax.sharding import PartitionSpec as P

SWEEPS = 4
SUBLANES = 8
MESH = pl.DeviceIdType.MESH
F32 = jnp.float32


def kernel(
    n, rows, cols,
    pert_hbm, probes_hbm, classes_hbm, rates_hbm, out,
    pert, probes, classes, rates,
    core, above, below, side, side_above, side_below,
    side_out, side_in, cls, cls_in, cls_above, cls_below,
    probe_field, keep, rate, turned, field_a, field_b, result, total,
    in_sem, z_send, z_recv, zs_send, zs_recv, y_send, y_recv, ys_send, ys_recv,
    x_send, x_recv, cx_send, cx_recv, cy_send, cy_recv,
):
    slabs, tile_rows, tile_cols = pert.shape
    pairs = slabs // 2
    half = tile_rows // 2
    wide = tile_cols + 128
    tall = tile_rows + half
    me = lax.axis_index("member")
    row = lax.axis_index("row")
    col = lax.axis_index("col")

    loads = [
        pltpu.make_async_copy(src, dst, in_sem.at[at])
        for at, (src, dst) in enumerate(
            ((pert_hbm, pert), (probes_hbm, probes), (classes_hbm, classes), (rates_hbm, rates))
        )
    ]
    for load in loads:
        load.start()

    has_up = (row + rows - 1) // rows
    has_down = 1 - (row + 1) // rows
    has_left = (col + cols - 1) // cols
    has_right = 1 - (col + 1) // cols
    has_prev = (me + n - 1) // n
    has_next = 1 - (me + 1) // n
    sides = (
        (has_up, {"row": row - 1}),
        (has_down, {"row": row + 1}),
        (has_left, {"col": col - 1}),
        (has_right, {"col": col + 1}),
        (has_prev, {"member": me - 1}),
        (has_next, {"member": me + 1}),
    )

    barrier = pltpu.get_barrier_semaphore()
    for has, where in sides:
        @pl.when(has == 1)
        def _(where=where):
            pl.semaphore_signal(barrier, inc=1, device_id=where, device_id_type=MESH)

    def remote(src, dst, send, recv, where):
        return pltpu.make_async_remote_copy(
            src_ref=src, dst_ref=dst, send_sem=send, recv_sem=recv,
            device_id=where, device_id_type=MESH,
        )

    def x_copies(at):
        where = sides[2 + at][1]
        block = (0, tile_cols - 128)[at]
        return (
            remote(side_out.at[at], side_in.at[at], x_send.at[at], x_recv.at[at], where),
            remote(classes.at[:, block : block + 128], cls_in.at[at], cx_send.at[at], cx_recv.at[at], where),
        )

    def z_copy(slot, pair, at):
        return remote(
            core.at[slot, pair], core.at[slot, pair],
            z_send.at[slot, pair, at], z_recv.at[slot, pair], sides[4 + at][1],
        )

    def zs_copy(slot, at):
        return remote(
            side.at[slot], side.at[slot], zs_send.at[slot, at], zs_recv.at[slot], sides[4 + at][1]
        )

    def y_copy(slot, pair, at):
        return remote(
            core.at[slot, pair, at], (below, above)[at].at[slot, pair],
            y_send.at[slot, pair, at], y_recv.at[slot, pair, at], sides[at][1],
        )

    def ys_copy(slot, at):
        return remote(
            side.at[slot], (side_below, side_above)[at].at[slot],
            ys_send.at[slot, at], ys_recv.at[slot, at], sides[at][1],
        )

    def cy_copy(at):
        return remote(
            cls.at[at * half : (at + 1) * half], (cls_below, cls_above)[at],
            cy_send.at[at], cy_recv.at[at], sides[at][1],
        )

    def if_sent(at):
        return pl.when(sides[at][0] == 1)

    fold = tile_cols // 2
    low_rows = lax.broadcasted_iota(jnp.int32, (half, tile_cols), 0) < half // 2
    low_side = lax.broadcasted_iota(jnp.int32, (half, 128), 0) < half // 2

    def swap(rows_now):
        return pltpu.roll(rows_now, half // 2, 0)

    def folded(rows_now):
        return jnp.concatenate([rows_now[:, :fold], rows_now[:, fold:]], 0).astype(jnp.bfloat16)

    def unfolded(block):
        both = block.astype(F32)
        return jnp.concatenate([both[:half], both[half:]], 1)

    def pack(which, slot):
        for pair in range(pairs):
            first = which[2 * pair].astype(F32)
            second = which[2 * pair + 1].astype(F32)
            core[slot, pair, 0] = folded(jnp.where(low_rows, first[:half], swap(second[:half])))
            core[slot, pair, 1] = folded(jnp.where(low_rows, swap(first[half:]), second[half:]))
            for at, tile in enumerate((first, second)):
                core[slot, pair, 2 + at] = folded(jnp.where(low_rows, swap(tile[:half]), swap(tile[half:])))

    def start_rows(slot):
        for pair in range(pairs):
            for at in range(2):
                @if_sent(at)
                def _(pair=pair, at=at):
                    y_copy(slot, pair, at).start()

    loads[0].wait()
    pack(pert, me)
    pl.semaphore_wait(barrier, has_up + has_down + has_left + has_right + has_prev + has_next)

    for pair in range(pairs):
        for at in range(2):
            @if_sent(4 + at)
            def _(pair=pair, at=at):
                z_copy(me, pair, at).start()

    for load in loads[1:]:
        load.wait()
    lane = lax.broadcasted_iota(jnp.int32, (tile_rows, 128), 1)
    for at, which in enumerate((pert, probes)):
        to_left = jnp.zeros((tile_rows, 128), F32)
        to_right = jnp.zeros((tile_rows, 128), F32)
        for slab in range(slabs):
            low = SWEEPS * slab
            head = which[slab, :, 0:128].astype(F32)
            tail = which[slab, :, tile_cols - 128 : tile_cols].astype(F32)
            if slab:
                head = pltpu.roll(head, low, 1)
                tail = pltpu.roll(tail, 128 - low, 1)
            to_left = jnp.where((lane >= low) & (lane < low + SWEEPS), head, to_left)
            to_right = jnp.where((lane >= 128 - SWEEPS - low) & (lane < 128 - low), tail, to_right)
        for way, rim in enumerate((to_left, to_right)):
            ends = jnp.where(low_side, rim[:half], rim[half:])
            middle = jnp.where(low_side, swap(rim[:half]), swap(rim[half:]))
            side_out[way, at] = jnp.concatenate([ends, middle], 0).astype(jnp.bfloat16)
    for at in range(2):
        @if_sent(2 + at)
        def _(at=at):
            for copy in x_copies(at):
                copy.start()

    pack(probes, n)
    start_rows(n)
    start_rows(me)
    cls[:, 0:tile_cols] = classes[...]

    @pl.when(has_up == 0)
    def _():
        above[...] = jnp.zeros_like(above)
        side_above[...] = jnp.zeros_like(side_above)
        cls_above[...] = jnp.full_like(cls_above, -1)

    @pl.when(has_down == 0)
    def _():
        below[...] = jnp.zeros_like(below)
        side_below[...] = jnp.zeros_like(side_below)
        cls_below[...] = jnp.full_like(cls_below, -1)

    @pl.when(has_right == 0)
    def _():
        side_in[0] = jnp.zeros_like(side_in[0])
        cls_in[0] = jnp.full_like(cls_in[0], -1)

    @pl.when(has_left == 0)
    def _():
        side_in[1] = jnp.zeros_like(side_in[1])
        cls_in[1] = jnp.full_like(cls_in[1], -1)

    for at in range(2):
        @if_sent(3 - at)
        def _(at=at):
            for copy in x_copies(at):
                copy.wait_recv()

    for at, slot in enumerate((me, n)):
        merged = jnp.where(lane < 64, side_in[0, at].astype(F32), side_in[1, at].astype(F32))
        side[slot] = merged.astype(jnp.bfloat16)
    cls[:, tile_cols:wide] = jnp.where(lane < 64, cls_in[0], cls_in[1])

    for slot in (n, me):
        for at in range(2):
            @if_sent(at)
            def _(slot=slot, at=at):
                ys_copy(slot, at).start()

    for at in range(2):
        @if_sent(at)
        def _(at=at):
            cy_copy(at).start()

    for at in range(2):
        @if_sent(4 + at)
        def _(at=at):
            zs_copy(me, at).start()

    lane_tall = lax.broadcasted_iota(jnp.int32, (tall, 128), 1) < 64

    def place(at):
        return at + half if at < 0 else at if at < half // 2 else at + half // 2

    def widened(slot, pair):
        top, bottom = unfolded(core[slot, pair, 0]), unfolded(core[slot, pair, 1])
        over, under = unfolded(above[slot, pair]), unfolded(below[slot, pair])
        beside_own = side[slot].astype(F32)
        ends, middle = beside_own[:half], beside_own[half:]
        beside = jnp.concatenate(
            [
                jnp.where(low_side, ends, side_above[slot].astype(F32)[:half]),
                middle,
                swap(jnp.where(low_side, side_below[slot].astype(F32)[:half], ends)),
            ],
            0,
        )
        both = []
        for at in range(2):
            low = SWEEPS * (2 * pair + at)
            if at == 0:
                head = jnp.where(low_rows, top, swap(over))
                tail = jnp.where(low_rows, bottom, swap(under))
            else:
                head = jnp.where(low_rows, swap(top), over)
                tail = jnp.where(low_rows, swap(bottom), under)
            mine = jnp.concatenate([head, unfolded(core[slot, pair, 2 + at]), tail], 0)
            end = jnp.where(
                lane_tall,
                pltpu.roll(beside, (128 - low) % 128, 1) if low else beside,
                pltpu.roll(beside, low, 1) if low else beside,
            )
            both.append(jnp.concatenate([mine, end], 1))
        return both

    def centre(slot, pair):
        top, bottom = unfolded(core[slot, pair, 0]), unfolded(core[slot, pair, 1])
        return [
            jnp.concatenate([ends, unfolded(core[slot, pair, 2 + at])], 0)
            for at, ends in enumerate(
                (jnp.where(low_rows, top, swap(bottom)), jnp.where(low_rows, swap(top), bottom))
            )
        ]

    def result_place(at):
        if at < half // 2:
            return at
        return at - half if at >= tile_rows - half // 2 else at + half // 2

    def y_arrival(slot, pair):
        for at in range(2):
            @if_sent(1 - at)
            def _(at=at):
                y_copy(slot, pair, at).wait_recv()

    def ys_arrival(slot):
        for at in range(2):
            @if_sent(1 - at)
            def _(at=at):
                ys_copy(slot, at).wait_recv()

    for at in range(2):
        @if_sent(1 - at)
        def _(at=at):
            cy_copy(at).wait_recv()

    low_cls = lax.broadcasted_iota(jnp.int32, (half, wide), 0) < half // 2
    kind = jnp.concatenate([cls[...], jnp.where(low_cls, cls_below[...], cls_above[...])], 0)
    picked = jnp.zeros((tall, wide), F32)
    for level in range(rates.shape[0]):
        picked = jnp.where(kind == level, rates[level], picked)
    for at in range(tall):
        line = jnp.broadcast_to(picked[at : at + 1], (SUBLANES, wide))
        rate[at] = line
        keep[at] = 1.0 - 4.0 * line

    ys_arrival(n)

    for pair in range(pairs):
        y_arrival(n, pair)
        for at, field in enumerate(widened(n, pair)):
            probe_field[2 * pair + at] = field
            total[2 * pair + at] = jnp.zeros((tile_rows, tile_cols), F32)

    blocks = wide // 128
    if slabs < SUBLANES:
        turned[:, slabs * tall :] = jnp.zeros((blocks, (SUBLANES - slabs) * tall, 128), F32)

    def sweep(load, store, margin):
        above_now, now = load(-margin - 1), load(-margin)
        for at in range(-margin, tile_rows + margin):
            below_now = load(at + 1)
            beside = above_now + below_now + pltpu.roll(now, 1, 1) + pltpu.roll(now, wide - 1, 1)
            store(at, keep[at % tall] * now + rate[at % tall] * beside)
            above_now, now = now, below_now

    def load_turned(at):
        picks = [
            turned[block, pl.ds(place(at), SUBLANES, stride=tall), :] for block in range(blocks)
        ]
        return jnp.concatenate(picks, 1)

    def store_result(at, value):
        for block in range(tile_cols // 128):
            result[block, pl.ds(result_place(at), SUBLANES, stride=tile_rows), :] = value[:, block * 128 : (block + 1) * 128]

    def through(buffer):
        def load(at):
            return buffer[at % tall]

        def store(at, value):
            buffer[at % tall] = value

        return load, store

    def add_member(slot):
        for pair in range(pairs):
            y_arrival(slot, pair)
        ys_arrival(slot)
        for pair in range(pairs):
            for at, member in enumerate(widened(slot, pair)):
                slab = 2 * pair + at
                field = member * probe_field[slab]
                for block in range(blocks):
                    turned[block, slab * tall : (slab + 1) * tall] = field[:, block * 128 : (block + 1) * 128]
        load_a, store_a = through(field_a)
        load_b, store_b = through(field_b)
        loads_now = load_turned
        for step in range(SWEEPS):
            store_now = store_result if step == SWEEPS - 1 else (store_a, store_b)[step % 2]
            sweep(loads_now, store_now, SWEEPS - 1 - step)
            loads_now = (load_a, load_b)[step % 2]
        for pair in range(pairs):
            for at, member in enumerate(centre(slot, pair)):
                slab = 2 * pair + at
                done = jnp.concatenate(
                    [result[block, slab * tile_rows : (slab + 1) * tile_rows] for block in range(tile_cols // 128)], 1
                )
                total[slab] += member * done

    def hand_on(slot, pair, onward):
        z_copy(slot, pair, onward).wait_recv()

        @if_sent(4 + onward)
        def _():
            z_copy(slot, pair, onward).start()

        for at in range(2):
            @if_sent(at)
            def _(at=at):
                y_copy(slot, pair, at).start()

    def hand_on_side(slot, onward):
        zs_copy(slot, onward).wait_recv()

        @if_sent(4 + onward)
        def _():
            zs_copy(slot, onward).start()

        for at in range(2):
            @if_sent(at)
            def _(at=at):
                ys_copy(slot, at).start()

    def at_distance(away, act):
        @pl.when(me - away >= 0)
        def _():
            act(me - away, 1)

        @pl.when(me + away < n)
        def _():
            act(me + away, 0)

    def arrivals(away):
        for pair in range(pairs):
            at_distance(away, lambda slot, onward: hand_on(slot, pair, onward))
        at_distance(away, hand_on_side)

    lower = 1 - (2 * me) // n

    @pl.loop(0, 2 * n)
    def _(turn):
        away = turn // 2
        second = turn % 2
        slot = me + away * (2 * ((second + lower) % 2) - 1)

        @pl.when(second == 1)
        def _():
            arrivals(away + 1)

        @pl.when((slot >= 0) & (slot < n) & (turn > 0))
        def _():
            add_member(slot)

    for slab in range(slabs):
        ends, middle = total[slab, :half], swap(total[slab, half:])
        out[slab, :half] = jnp.where(low_rows, ends, middle)
        out[slab, half:] = jnp.where(low_rows, middle, ends)

    @pl.loop(0, n)
    def _(slot):
        for at in range(2):
            @pl.when((sides[4 + at][0] == 1) & ((slot >= me) if at == 0 else (slot <= me)))
            def _(at=at):
                for pair in range(pairs):
                    z_copy(slot, pair, at).wait_send()
                zs_copy(slot, at).wait_send()

    @pl.loop(0, n + 1)
    def _(slot):
        for at in range(2):
            @if_sent(at)
            def _(at=at):
                for pair in range(pairs):
                    y_copy(slot, pair, at).wait_send()
                ys_copy(slot, at).wait_send()

    for at in range(2):
        @if_sent(at)
        def _(at=at):
            cy_copy(at).wait_send()

        @if_sent(2 + at)
        def _(at=at):
            for copy in x_copies(at):
                copy.wait_send()


def body(n, rows, cols, pert, probes, diff_class, class_rate):
    mem_local, variables, levels, tile_rows, tile_cols = pert.shape
    slabs = variables * levels
    pairs = slabs // 2
    half = tile_rows // 2
    wide = tile_cols + 128
    tall = tile_rows + half
    bf16 = jnp.bfloat16
    flat = (slabs, tile_rows, tile_cols)
    vmem = pl.BlockSpec(memory_space=pltpu.VMEM)
    dma = pltpu.SemaphoreType.DMA
    out = pl.pallas_call(
        functools.partial(kernel, n, rows, cols),
        out_shape=pltpu.VMEM(flat, F32),
        in_specs=[pl.BlockSpec(memory_space=pltpu.HBM)] * 4,
        out_specs=vmem,
        scratch_shapes=[
            pltpu.VMEM(flat, bf16),
            pltpu.VMEM(flat, bf16),
            pltpu.VMEM((tile_rows, tile_cols), jnp.int32),
            pltpu.SMEM(class_rate.shape, F32),
            pltpu.VMEM((n + 1, pairs, 4, tile_rows, tile_cols // 2), bf16),
            pltpu.VMEM((n + 1, pairs, tile_rows, tile_cols // 2), bf16),
            pltpu.VMEM((n + 1, pairs, tile_rows, tile_cols // 2), bf16),
            pltpu.VMEM((n + 1, tile_rows, 128), bf16),
            pltpu.VMEM((n + 1, tile_rows, 128), bf16),
            pltpu.VMEM((n + 1, tile_rows, 128), bf16),
            pltpu.VMEM((2, 2, tile_rows, 128), bf16),
            pltpu.VMEM((2, 2, tile_rows, 128), bf16),
            pltpu.VMEM((tile_rows, wide), jnp.int32),
            pltpu.VMEM((2, tile_rows, 128), jnp.int32),
            pltpu.VMEM((half, wide), jnp.int32),
            pltpu.VMEM((half, wide), jnp.int32),
            pltpu.VMEM((slabs, tall, wide), F32),
            pltpu.VMEM((tall, SUBLANES, wide), F32),
            pltpu.VMEM((tall, SUBLANES, wide), F32),
            pltpu.VMEM((wide // 128, SUBLANES * tall, 128), F32),
            pltpu.VMEM((tall, SUBLANES, wide), F32),
            pltpu.VMEM((tall, SUBLANES, wide), F32),
            pltpu.VMEM((tile_cols // 128, SUBLANES * tile_rows, 128), F32),
            pltpu.VMEM(flat, F32),
            dma((4,)), dma((n, pairs, 2)), dma((n, pairs)), dma((n, 2)), dma((n,)),
            dma((n + 1, pairs, 2)), dma((n + 1, pairs, 2)), dma((n + 1, 2)), dma((n + 1, 2)),
            dma((2,)), dma((2,)), dma((2,)), dma((2,)), dma((2,)), dma((2,)),
        ],
        compiler_params=pltpu.CompilerParams(
            collective_id=0, has_side_effects=True, vmem_limit_bytes=60 * 1024 * 1024
        ),
    )(pert.reshape(flat), probes.reshape(flat), diff_class, class_rate)
    return out.reshape(pert.shape) / (n - 1)


def solution(mesh):
    placed = (
        P("member", None, None, "row", "col"),
        P("member", None, None, "row", "col"),
        P("row", "col"),
        P(),
    )
    sizes = (mesh.shape["member"], mesh.shape["row"], mesh.shape["col"])
    return jax.shard_map(
        functools.partial(body, *sizes),
        mesh=mesh,
        in_specs=placed,
        out_specs=P("member", None, None, "row", "col"),
        check_vma=False,
    )
```

```python
import functools

import jax
import jax.numpy as jnp
from jax import lax
from jax.experimental import pallas as pl
from jax.experimental.pallas import tpu as pltpu
from jax.sharding import PartitionSpec as P

SWEEPS = 4
SUBLANES = 8
MESH = pl.DeviceIdType.MESH
F32 = jnp.float32


def kernel(
    n, rows, cols,
    pert_hbm, probes_hbm, classes_hbm, rates_hbm, out,
    pert, probes, classes, rates,
    core, above, below, side, side_above, side_below,
    side_out, side_in, cls, cls_in, cls_above, cls_below,
    probe_field, keep, rate, turned, field_a, field_b, result, total,
    in_sem, z_send, z_recv, zs_send, zs_recv, y_send, y_recv, ys_send, ys_recv,
    x_send, x_recv, cx_send, cx_recv, cy_send, cy_recv,
):
    slabs, tile_rows, tile_cols = pert.shape
    pairs = slabs // 2
    half = tile_rows // 2
    wide = tile_cols + 128
    tall = tile_rows + half
    me = lax.axis_index("member")
    row = lax.axis_index("row")
    col = lax.axis_index("col")

    loads = [
        pltpu.make_async_copy(src, dst, in_sem.at[at])
        for at, (src, dst) in enumerate(
            ((pert_hbm, pert), (probes_hbm, probes), (classes_hbm, classes), (rates_hbm, rates))
        )
    ]
    for load in loads:
        load.start()

    has_up = (row + rows - 1) // rows
    has_down = 1 - (row + 1) // rows
    has_left = (col + cols - 1) // cols
    has_right = 1 - (col + 1) // cols
    has_prev = (me + n - 1) // n
    has_next = 1 - (me + 1) // n
    sides = (
        (has_up, {"row": row - 1}),
        (has_down, {"row": row + 1}),
        (has_left, {"col": col - 1}),
        (has_right, {"col": col + 1}),
        (has_prev, {"member": me - 1}),
        (has_next, {"member": me + 1}),
    )

    barrier = pltpu.get_barrier_semaphore()
    for has, where in sides:
        @pl.when(has == 1)
        def _(where=where):
            pl.semaphore_signal(barrier, inc=1, device_id=where, device_id_type=MESH)

    def remote(src, dst, send, recv, where):
        return pltpu.make_async_remote_copy(
            src_ref=src, dst_ref=dst, send_sem=send, recv_sem=recv,
            device_id=where, device_id_type=MESH,
        )

    def x_copies(at):
        where = sides[2 + at][1]
        block = (0, tile_cols - 128)[at]
        return (
            remote(side_out.at[at], side_in.at[at], x_send.at[at], x_recv.at[at], where),
            remote(classes.at[:, block : block + 128], cls_in.at[at], cx_send.at[at], cx_recv.at[at], where),
        )

    def z_copy(slot, pair, at):
        return remote(
            core.at[slot, pair], core.at[slot, pair],
            z_send.at[slot, pair, at], z_recv.at[slot, pair], sides[4 + at][1],
        )

    def zs_copy(slot, at):
        return remote(
            side.at[slot], side.at[slot], zs_send.at[slot, at], zs_recv.at[slot], sides[4 + at][1]
        )

    def y_copy(slot, pair, at):
        return remote(
            core.at[slot, pair, at], (below, above)[at].at[slot, pair],
            y_send.at[slot, pair, at], y_recv.at[slot, pair, at], sides[at][1],
        )

    def ys_copy(slot, at):
        return remote(
            side.at[slot], (side_below, side_above)[at].at[slot],
            ys_send.at[slot, at], ys_recv.at[slot, at], sides[at][1],
        )

    def cy_copy(at):
        return remote(
            cls.at[at * half : (at + 1) * half], (cls_below, cls_above)[at],
            cy_send.at[at], cy_recv.at[at], sides[at][1],
        )

    def if_sent(at):
        return pl.when(sides[at][0] == 1)

    fold = tile_cols // 2
    low_rows = lax.broadcasted_iota(jnp.int32, (half, tile_cols), 0) < half // 2
    low_side = lax.broadcasted_iota(jnp.int32, (half, 128), 0) < half // 2

    def swap(rows_now):
        return pltpu.roll(rows_now, half // 2, 0)

    def folded(rows_now):
        return jnp.concatenate([rows_now[:, :fold], rows_now[:, fold:]], 0).astype(jnp.bfloat16)

    def unfolded(block):
        both = block.astype(F32)
        return jnp.concatenate([both[:half], both[half:]], 1)

    def pack(which, slot):
        for pair in range(pairs):
            first = which[2 * pair].astype(F32)
            second = which[2 * pair + 1].astype(F32)
            core[slot, pair, 0] = folded(jnp.where(low_rows, first[:half], swap(second[:half])))
            core[slot, pair, 1] = folded(jnp.where(low_rows, swap(first[half:]), second[half:]))
            for at, tile in enumerate((first, second)):
                core[slot, pair, 2 + at] = folded(jnp.where(low_rows, swap(tile[:half]), swap(tile[half:])))

    def start_rows(slot):
        for pair in range(pairs):
            for at in range(2):
                @if_sent(at)
                def _(pair=pair, at=at):
                    y_copy(slot, pair, at).start()

    loads[0].wait()
    pack(pert, me)
    pl.semaphore_wait(barrier, has_up + has_down + has_left + has_right + has_prev + has_next)

    for pair in range(pairs):
        for at in range(2):
            @if_sent(4 + at)
            def _(pair=pair, at=at):
                z_copy(me, pair, at).start()

    for load in loads[1:]:
        load.wait()
    lane = lax.broadcasted_iota(jnp.int32, (tile_rows, 128), 1)
    for at, which in enumerate((pert, probes)):
        to_left = jnp.zeros((tile_rows, 128), F32)
        to_right = jnp.zeros((tile_rows, 128), F32)
        for slab in range(slabs):
            low = SWEEPS * slab
            head = which[slab, :, 0:128].astype(F32)
            tail = which[slab, :, tile_cols - 128 : tile_cols].astype(F32)
            if slab:
                head = pltpu.roll(head, low, 1)
                tail = pltpu.roll(tail, 128 - low, 1)
            to_left = jnp.where((lane >= low) & (lane < low + SWEEPS), head, to_left)
            to_right = jnp.where((lane >= 128 - SWEEPS - low) & (lane < 128 - low), tail, to_right)
        for way, rim in enumerate((to_left, to_right)):
            ends = jnp.where(low_side, rim[:half], rim[half:])
            middle = jnp.where(low_side, swap(rim[:half]), swap(rim[half:]))
            side_out[way, at] = jnp.concatenate([ends, middle], 0).astype(jnp.bfloat16)
    for at in range(2):
        @if_sent(2 + at)
        def _(at=at):
            for copy in x_copies(at):
                copy.start()

    pack(probes, n)
    start_rows(n)
    start_rows(me)
    cls[:, 0:tile_cols] = classes[...]

    @pl.when(has_up == 0)
    def _():
        above[...] = jnp.zeros_like(above)
        side_above[...] = jnp.zeros_like(side_above)
        cls_above[...] = jnp.full_like(cls_above, -1)

    @pl.when(has_down == 0)
    def _():
        below[...] = jnp.zeros_like(below)
        side_below[...] = jnp.zeros_like(side_below)
        cls_below[...] = jnp.full_like(cls_below, -1)

    @pl.when(has_right == 0)
    def _():
        side_in[0] = jnp.zeros_like(side_in[0])
        cls_in[0] = jnp.full_like(cls_in[0], -1)

    @pl.when(has_left == 0)
    def _():
        side_in[1] = jnp.zeros_like(side_in[1])
        cls_in[1] = jnp.full_like(cls_in[1], -1)

    for at in range(2):
        @if_sent(3 - at)
        def _(at=at):
            for copy in x_copies(at):
                copy.wait_recv()

    for at, slot in enumerate((me, n)):
        merged = jnp.where(lane < 64, side_in[0, at].astype(F32), side_in[1, at].astype(F32))
        side[slot] = merged.astype(jnp.bfloat16)
    cls[:, tile_cols:wide] = jnp.where(lane < 64, cls_in[0], cls_in[1])

    for slot in (n, me):
        for at in range(2):
            @if_sent(at)
            def _(slot=slot, at=at):
                ys_copy(slot, at).start()

    for at in range(2):
        @if_sent(at)
        def _(at=at):
            cy_copy(at).start()

    for at in range(2):
        @if_sent(4 + at)
        def _(at=at):
            zs_copy(me, at).start()

    lane_tall = lax.broadcasted_iota(jnp.int32, (tall, 128), 1) < 64

    def place(at):
        return at + half if at < 0 else at if at < half // 2 else at + half // 2

    def widened(slot, pair):
        top, bottom = unfolded(core[slot, pair, 0]), unfolded(core[slot, pair, 1])
        over, under = unfolded(above[slot, pair]), unfolded(below[slot, pair])
        beside_own = side[slot].astype(F32)
        ends, middle = beside_own[:half], beside_own[half:]
        beside = jnp.concatenate(
            [
                jnp.where(low_side, ends, side_above[slot].astype(F32)[:half]),
                middle,
                swap(jnp.where(low_side, side_below[slot].astype(F32)[:half], ends)),
            ],
            0,
        )
        both = []
        for at in range(2):
            low = SWEEPS * (2 * pair + at)
            if at == 0:
                head = jnp.where(low_rows, top, swap(over))
                tail = jnp.where(low_rows, bottom, swap(under))
            else:
                head = jnp.where(low_rows, swap(top), over)
                tail = jnp.where(low_rows, swap(bottom), under)
            mine = jnp.concatenate([head, unfolded(core[slot, pair, 2 + at]), tail], 0)
            end = jnp.where(
                lane_tall,
                pltpu.roll(beside, (128 - low) % 128, 1) if low else beside,
                pltpu.roll(beside, low, 1) if low else beside,
            )
            both.append(jnp.concatenate([mine, end], 1))
        return both

    def centre(slot, pair):
        top, bottom = unfolded(core[slot, pair, 0]), unfolded(core[slot, pair, 1])
        return [
            jnp.concatenate([ends, unfolded(core[slot, pair, 2 + at])], 0)
            for at, ends in enumerate(
                (jnp.where(low_rows, top, swap(bottom)), jnp.where(low_rows, swap(top), bottom))
            )
        ]

    def result_place(at):
        if at < half // 2:
            return at
        return at - half if at >= tile_rows - half // 2 else at + half // 2

    def y_arrival(slot, pair):
        for at in range(2):
            @if_sent(1 - at)
            def _(at=at):
                y_copy(slot, pair, at).wait_recv()

    def ys_arrival(slot):
        for at in range(2):
            @if_sent(1 - at)
            def _(at=at):
                ys_copy(slot, at).wait_recv()

    for at in range(2):
        @if_sent(1 - at)
        def _(at=at):
            cy_copy(at).wait_recv()

    low_cls = lax.broadcasted_iota(jnp.int32, (half, wide), 0) < half // 2
    kind = jnp.concatenate([cls[...], jnp.where(low_cls, cls_below[...], cls_above[...])], 0)
    picked = jnp.zeros((tall, wide), F32)
    for level in range(rates.shape[0]):
        picked = jnp.where(kind == level, rates[level], picked)
    for at in range(tall):
        line = jnp.broadcast_to(picked[at : at + 1], (SUBLANES, wide))
        rate[at] = line
        keep[at] = 1.0 - 4.0 * line

    ys_arrival(n)

    for pair in range(pairs):
        y_arrival(n, pair)
        for at, field in enumerate(widened(n, pair)):
            probe_field[2 * pair + at] = field
            total[2 * pair + at] = jnp.zeros((tile_rows, tile_cols), F32)

    blocks = wide // 128
    if slabs < SUBLANES:
        turned[:, slabs * tall :] = jnp.zeros((blocks, (SUBLANES - slabs) * tall, 128), F32)

    def sweep(load, store, margin):
        above_now, now = load(-margin - 1), load(-margin)
        for at in range(-margin, tile_rows + margin):
            below_now = load(at + 1)
            beside = above_now + below_now + pltpu.roll(now, 1, 1) + pltpu.roll(now, wide - 1, 1)
            store(at, keep[at % tall] * now + rate[at % tall] * beside)
            above_now, now = now, below_now

    def load_turned(at):
        picks = [
            turned[block, pl.ds(place(at), SUBLANES, stride=tall), :] for block in range(blocks)
        ]
        return jnp.concatenate(picks, 1)

    def store_result(at, value):
        for block in range(tile_cols // 128):
            result[block, pl.ds(result_place(at), SUBLANES, stride=tile_rows), :] = value[:, block * 128 : (block + 1) * 128]

    def through(buffer):
        def load(at):
            return buffer[at % tall]

        def store(at, value):
            buffer[at % tall] = value

        return load, store

    def add_member(slot):
        for pair in range(pairs):
            y_arrival(slot, pair)
        ys_arrival(slot)
        for pair in range(pairs):
            for at, member in enumerate(widened(slot, pair)):
                slab = 2 * pair + at
                field = member * probe_field[slab]
                for block in range(blocks):
                    turned[block, slab * tall : (slab + 1) * tall] = field[:, block * 128 : (block + 1) * 128]
        load_a, store_a = through(field_a)
        load_b, store_b = through(field_b)
        loads_now = load_turned
        for step in range(SWEEPS):
            store_now = store_result if step == SWEEPS - 1 else (store_a, store_b)[step % 2]
            sweep(loads_now, store_now, SWEEPS - 1 - step)
            loads_now = (load_a, load_b)[step % 2]
        for pair in range(pairs):
            for at, member in enumerate(centre(slot, pair)):
                slab = 2 * pair + at
                done = jnp.concatenate(
                    [result[block, slab * tile_rows : (slab + 1) * tile_rows] for block in range(tile_cols // 128)], 1
                )
                total[slab] += member * done

    def hand_on(slot, pair, onward):
        z_copy(slot, pair, onward).wait_recv()

        @if_sent(4 + onward)
        def _():
            z_copy(slot, pair, onward).start()

        for at in range(2):
            @if_sent(at)
            def _(at=at):
                y_copy(slot, pair, at).start()

    def hand_on_side(slot, onward):
        zs_copy(slot, onward).wait_recv()

        @if_sent(4 + onward)
        def _():
            zs_copy(slot, onward).start()

        for at in range(2):
            @if_sent(at)
            def _(at=at):
                ys_copy(slot, at).start()

    def at_distance(away, act):
        @pl.when(me - away >= 0)
        def _():
            act(me - away, 1)

        @pl.when(me + away < n)
        def _():
            act(me + away, 0)

    def arrivals(away):
        for pair in range(pairs):
            at_distance(away, lambda slot, onward: hand_on(slot, pair, onward))
        at_distance(away, hand_on_side)

    lower = 1 - (2 * me) // n
    ahead = has_prev + has_next

    @pl.when(ahead == 2)
    def _():
        arrivals(1)

    @pl.loop(0, 2 * n)
    def _(turn):
        away = turn // 2
        second = turn % 2
        slot = me + away * (2 * ((second + lower) % 2) - 1)

        @pl.when(second == 1)
        def _():
            arrivals(away + ahead)

        @pl.when((slot >= 0) & (slot < n) & (turn > 0))
        def _():
            add_member(slot)

    for slab in range(slabs):
        ends, middle = total[slab, :half], swap(total[slab, half:])
        out[slab, :half] = jnp.where(low_rows, ends, middle)
        out[slab, half:] = jnp.where(low_rows, middle, ends)

    @pl.loop(0, n)
    def _(slot):
        for at in range(2):
            @pl.when((sides[4 + at][0] == 1) & ((slot >= me) if at == 0 else (slot <= me)))
            def _(at=at):
                for pair in range(pairs):
                    z_copy(slot, pair, at).wait_send()
                zs_copy(slot, at).wait_send()

    @pl.loop(0, n + 1)
    def _(slot):
        for at in range(2):
            @if_sent(at)
            def _(at=at):
                for pair in range(pairs):
                    y_copy(slot, pair, at).wait_send()
                ys_copy(slot, at).wait_send()

    for at in range(2):
        @if_sent(at)
        def _(at=at):
            cy_copy(at).wait_send()

        @if_sent(2 + at)
        def _(at=at):
            for copy in x_copies(at):
                copy.wait_send()


def body(n, rows, cols, pert, probes, diff_class, class_rate):
    mem_local, variables, levels, tile_rows, tile_cols = pert.shape
    slabs = variables * levels
    pairs = slabs // 2
    half = tile_rows // 2
    wide = tile_cols + 128
    tall = tile_rows + half
    bf16 = jnp.bfloat16
    flat = (slabs, tile_rows, tile_cols)
    vmem = pl.BlockSpec(memory_space=pltpu.VMEM)
    dma = pltpu.SemaphoreType.DMA
    out = pl.pallas_call(
        functools.partial(kernel, n, rows, cols),
        out_shape=pltpu.VMEM(flat, F32),
        in_specs=[pl.BlockSpec(memory_space=pltpu.HBM)] * 4,
        out_specs=vmem,
        scratch_shapes=[
            pltpu.VMEM(flat, bf16),
            pltpu.VMEM(flat, bf16),
            pltpu.VMEM((tile_rows, tile_cols), jnp.int32),
            pltpu.SMEM(class_rate.shape, F32),
            pltpu.VMEM((n + 1, pairs, 4, tile_rows, tile_cols // 2), bf16),
            pltpu.VMEM((n + 1, pairs, tile_rows, tile_cols // 2), bf16),
            pltpu.VMEM((n + 1, pairs, tile_rows, tile_cols // 2), bf16),
            pltpu.VMEM((n + 1, tile_rows, 128), bf16),
            pltpu.VMEM((n + 1, tile_rows, 128), bf16),
            pltpu.VMEM((n + 1, tile_rows, 128), bf16),
            pltpu.VMEM((2, 2, tile_rows, 128), bf16),
            pltpu.VMEM((2, 2, tile_rows, 128), bf16),
            pltpu.VMEM((tile_rows, wide), jnp.int32),
            pltpu.VMEM((2, tile_rows, 128), jnp.int32),
            pltpu.VMEM((half, wide), jnp.int32),
            pltpu.VMEM((half, wide), jnp.int32),
            pltpu.VMEM((slabs, tall, wide), F32),
            pltpu.VMEM((tall, SUBLANES, wide), F32),
            pltpu.VMEM((tall, SUBLANES, wide), F32),
            pltpu.VMEM((wide // 128, SUBLANES * tall, 128), F32),
            pltpu.VMEM((tall, SUBLANES, wide), F32),
            pltpu.VMEM((tall, SUBLANES, wide), F32),
            pltpu.VMEM((tile_cols // 128, SUBLANES * tile_rows, 128), F32),
            pltpu.VMEM(flat, F32),
            dma((4,)), dma((n, pairs, 2)), dma((n, pairs)), dma((n, 2)), dma((n,)),
            dma((n + 1, pairs, 2)), dma((n + 1, pairs, 2)), dma((n + 1, 2)), dma((n + 1, 2)),
            dma((2,)), dma((2,)), dma((2,)), dma((2,)), dma((2,)), dma((2,)),
        ],
        compiler_params=pltpu.CompilerParams(
            collective_id=0, has_side_effects=True, vmem_limit_bytes=60 * 1024 * 1024
        ),
    )(pert.reshape(flat), probes.reshape(flat), diff_class, class_rate)
    return out.reshape(pert.shape) / (n - 1)


def solution(mesh):
    placed = (
        P("member", None, None, "row", "col"),
        P("member", None, None, "row", "col"),
        P("row", "col"),
        P(),
    )
    sizes = (mesh.shape["member"], mesh.shape["row"], mesh.shape["col"])
    return jax.shard_map(
        functools.partial(body, *sizes),
        mesh=mesh,
        in_specs=placed,
        out_specs=P("member", None, None, "row", "col"),
        check_vma=False,
    )
```

```python
import functools

import jax
import jax.numpy as jnp
from jax import lax
from jax.experimental import pallas as pl
from jax.experimental.pallas import tpu as pltpu
from jax.sharding import PartitionSpec as P

SWEEPS = 4
SUBLANES = 8
MESH = pl.DeviceIdType.MESH
F32 = jnp.float32


def kernel(
    n, rows, cols,
    pert_hbm, probes_hbm, classes_hbm, rates_hbm, out,
    pert, probes, classes, rates,
    core, above, below,
    side_out, side_in, cls, cls_in, cls_above, cls_below,
    probe_field, keep, rate, turned, field_a, field_b, result, total,
    in_sem, z_send, z_recv, y_send, y_recv,
    x_send, x_recv, cx_send, cx_recv, cy_send, cy_recv,
):
    slabs, tile_rows, tile_cols = pert.shape
    pairs = slabs // 2
    half = tile_rows // 2
    wide = tile_cols + 128
    tall = tile_rows + half
    me = lax.axis_index("member")
    row = lax.axis_index("row")
    col = lax.axis_index("col")

    loads = [
        pltpu.make_async_copy(src, dst, in_sem.at[at])
        for at, (src, dst) in enumerate(
            ((pert_hbm, pert), (probes_hbm, probes), (classes_hbm, classes), (rates_hbm, rates))
        )
    ]
    for load in loads:
        load.start()

    has_up = (row + rows - 1) // rows
    has_down = 1 - (row + 1) // rows
    has_left = (col + cols - 1) // cols
    has_right = 1 - (col + 1) // cols
    has_prev = (me + n - 1) // n
    has_next = 1 - (me + 1) // n
    sides = (
        (has_up, {"row": row - 1}),
        (has_down, {"row": row + 1}),
        (has_left, {"col": col - 1}),
        (has_right, {"col": col + 1}),
        (has_prev, {"member": me - 1}),
        (has_next, {"member": me + 1}),
    )

    barrier = pltpu.get_barrier_semaphore()
    for has, where in sides:
        @pl.when(has == 1)
        def _(where=where):
            pl.semaphore_signal(barrier, inc=1, device_id=where, device_id_type=MESH)

    def remote(src, dst, send, recv, where):
        return pltpu.make_async_remote_copy(
            src_ref=src, dst_ref=dst, send_sem=send, recv_sem=recv,
            device_id=where, device_id_type=MESH,
        )

    def x_copies(at):
        where = sides[2 + at][1]
        block = (0, tile_cols - 128)[at]
        return (
            remote(side_out.at[at], side_in.at[at], x_send.at[at], x_recv.at[at], where),
            remote(classes.at[:, block : block + 128], cls_in.at[at], cx_send.at[at], cx_recv.at[at], where),
        )

    side_at = pairs * tile_rows
    bottom_at = side_at + tile_rows
    middle_at = bottom_at + side_at
    parts = (pl.ds(middle_at, slabs * tile_rows), pl.ds(0, middle_at))
    halo = side_at + tile_rows

    def z_copy(slot, part, at):
        return remote(
            core.at[slot, parts[part]], core.at[slot, parts[part]],
            z_send.at[slot, part, at], z_recv.at[slot, part], sides[4 + at][1],
        )

    def y_copy(slot, at):
        return remote(
            core.at[slot, pl.ds((0, side_at)[at], halo)], (below, above)[at].at[slot],
            y_send.at[slot, at], y_recv.at[slot, at], sides[at][1],
        )

    def cy_copy(at):
        return remote(
            cls.at[at * half : (at + 1) * half], (cls_below, cls_above)[at],
            cy_send.at[at], cy_recv.at[at], sides[at][1],
        )

    def if_sent(at):
        return pl.when(sides[at][0] == 1)

    fold = tile_cols // 2
    low_rows = lax.broadcasted_iota(jnp.int32, (half, tile_cols), 0) < half // 2
    low_side = lax.broadcasted_iota(jnp.int32, (half, 128), 0) < half // 2

    def swap(rows_now):
        return pltpu.roll(rows_now, half // 2, 0)

    def keep_block(slot, first, rows_now):
        both = jnp.concatenate([rows_now[:, :fold], rows_now[:, fold:]], 0)
        core[slot, first : first + tile_rows] = both.astype(jnp.bfloat16)

    def block_of(ref, slot, first):
        both = ref[slot, first : first + tile_rows].astype(F32)
        return jnp.concatenate([both[:half], both[half:]], 1)

    def pack(which, slot):
        for pair in range(pairs):
            first = which[2 * pair].astype(F32)
            second = which[2 * pair + 1].astype(F32)
            keep_block(slot, tile_rows * pair, jnp.where(low_rows, first[:half], swap(second[:half])))
            keep_block(slot, bottom_at + tile_rows * pair, jnp.where(low_rows, swap(first[half:]), second[half:]))
            for at, tile in enumerate((first, second)):
                keep_block(slot, middle_at + tile_rows * (2 * pair + at), jnp.where(low_rows, swap(tile[:half]), swap(tile[half:])))

    def start_rows(slot):
        for at in range(2):
            @if_sent(at)
            def _(at=at):
                y_copy(slot, at).start()

    loads[0].wait()
    pack(pert, me)
    pl.semaphore_wait(barrier, has_up + has_down + has_left + has_right + has_prev + has_next)

    for at in range(2):
        @if_sent(4 + at)
        def _(at=at):
            z_copy(me, 0, at).start()

    for load in loads[1:]:
        load.wait()
    lane = lax.broadcasted_iota(jnp.int32, (tile_rows, 128), 1)
    for at, which in enumerate((pert, probes)):
        to_left = jnp.zeros((tile_rows, 128), F32)
        to_right = jnp.zeros((tile_rows, 128), F32)
        for slab in range(slabs):
            low = SWEEPS * slab
            head = which[slab, :, 0:128].astype(F32)
            tail = which[slab, :, tile_cols - 128 : tile_cols].astype(F32)
            if slab:
                head = pltpu.roll(head, low, 1)
                tail = pltpu.roll(tail, 128 - low, 1)
            to_left = jnp.where((lane >= low) & (lane < low + SWEEPS), head, to_left)
            to_right = jnp.where((lane >= 128 - SWEEPS - low) & (lane < 128 - low), tail, to_right)
        for way, rim in enumerate((to_left, to_right)):
            ends = jnp.where(low_side, rim[:half], rim[half:])
            middle = jnp.where(low_side, swap(rim[:half]), swap(rim[half:]))
            side_out[way, at] = jnp.concatenate([ends, middle], 0).astype(jnp.bfloat16)
    for at in range(2):
        @if_sent(2 + at)
        def _(at=at):
            for copy in x_copies(at):
                copy.start()

    pack(probes, n)
    cls[:, 0:tile_cols] = classes[...]

    @pl.when(has_up == 0)
    def _():
        above[...] = jnp.zeros_like(above)
        cls_above[...] = jnp.full_like(cls_above, -1)

    @pl.when(has_down == 0)
    def _():
        below[...] = jnp.zeros_like(below)
        cls_below[...] = jnp.full_like(cls_below, -1)

    @pl.when(has_right == 0)
    def _():
        side_in[0] = jnp.zeros_like(side_in[0])
        cls_in[0] = jnp.full_like(cls_in[0], -1)

    @pl.when(has_left == 0)
    def _():
        side_in[1] = jnp.zeros_like(side_in[1])
        cls_in[1] = jnp.full_like(cls_in[1], -1)

    for at in range(2):
        @if_sent(3 - at)
        def _(at=at):
            for copy in x_copies(at):
                copy.wait_recv()

    for at, slot in enumerate((me, n)):
        merged = jnp.where(lane < 64, side_in[0, at].astype(F32), side_in[1, at].astype(F32))
        core[slot, side_at:bottom_at] = jnp.concatenate([merged] * (fold // 128), 1).astype(jnp.bfloat16)

    for at in range(2):
        @if_sent(4 + at)
        def _(at=at):
            z_copy(me, 1, at).start()
    start_rows(n)
    start_rows(me)

    cls[:, tile_cols:wide] = jnp.where(lane < 64, cls_in[0], cls_in[1])
    for at in range(2):
        @if_sent(at)
        def _(at=at):
            cy_copy(at).start()

    lane_tall = lax.broadcasted_iota(jnp.int32, (tall, 128), 1) < 64

    def place(at):
        return at + half if at < 0 else at if at < half // 2 else at + half // 2

    def top_of(slot, pair):
        return block_of(core, slot, tile_rows * pair)

    def bottom_of(slot, pair):
        return block_of(core, slot, bottom_at + tile_rows * pair)

    def middle_of(slot, pair, at):
        return block_of(core, slot, middle_at + tile_rows * (2 * pair + at))

    def widened(slot, pair):
        top, bottom = top_of(slot, pair), bottom_of(slot, pair)
        over = block_of(above, slot, tile_rows * (1 + pair))
        under = block_of(below, slot, tile_rows * pair)
        beside_own = core[slot, side_at:bottom_at, 0:128].astype(F32)
        ends, middle = beside_own[:half], beside_own[half:]
        beside = jnp.concatenate(
            [
                jnp.where(low_side, ends, above[slot, 0:tile_rows, 0:128].astype(F32)[:half]),
                middle,
                swap(jnp.where(low_side, below[slot, side_at:halo, 0:128].astype(F32)[:half], ends)),
            ],
            0,
        )
        both = []
        for at in range(2):
            low = SWEEPS * (2 * pair + at)
            if at == 0:
                head = jnp.where(low_rows, top, swap(over))
                tail = jnp.where(low_rows, bottom, swap(under))
            else:
                head = jnp.where(low_rows, swap(top), over)
                tail = jnp.where(low_rows, swap(bottom), under)
            mine = jnp.concatenate([head, middle_of(slot, pair, at), tail], 0)
            end = jnp.where(
                lane_tall,
                pltpu.roll(beside, (128 - low) % 128, 1) if low else beside,
                pltpu.roll(beside, low, 1) if low else beside,
            )
            both.append(jnp.concatenate([mine, end], 1))
        return both

    def centre(slot, pair):
        top, bottom = top_of(slot, pair), bottom_of(slot, pair)
        return [
            jnp.concatenate([ends, middle_of(slot, pair, at)], 0)
            for at, ends in enumerate(
                (jnp.where(low_rows, top, swap(bottom)), jnp.where(low_rows, swap(top), bottom))
            )
        ]

    def result_place(at):
        if at < half // 2:
            return at
        return at - half if at >= tile_rows - half // 2 else at + half // 2

    def y_arrival(slot):
        for at in range(2):
            @if_sent(1 - at)
            def _(at=at):
                y_copy(slot, at).wait_recv()

    for at in range(2):
        @if_sent(1 - at)
        def _(at=at):
            cy_copy(at).wait_recv()

    low_cls = lax.broadcasted_iota(jnp.int32, (half, wide), 0) < half // 2
    kind = jnp.concatenate([cls[...], jnp.where(low_cls, cls_below[...], cls_above[...])], 0)
    picked = jnp.zeros((tall, wide), F32)
    for level in range(rates.shape[0]):
        picked = jnp.where(kind == level, rates[level], picked)
    for at in range(tall):
        line = jnp.broadcast_to(picked[at : at + 1], (SUBLANES, wide))
        rate[at] = line
        keep[at] = 1.0 - 4.0 * line

    y_arrival(n)
    for pair in range(pairs):
        for at, field in enumerate(widened(n, pair)):
            probe_field[2 * pair + at] = field
            total[2 * pair + at] = jnp.zeros((tile_rows, tile_cols), F32)

    blocks = wide // 128
    if slabs < SUBLANES:
        turned[:, slabs * tall :] = jnp.zeros((blocks, (SUBLANES - slabs) * tall, 128), F32)

    def sweep(load, store, margin):
        above_now, now = load(-margin - 1), load(-margin)
        for at in range(-margin, tile_rows + margin):
            below_now = load(at + 1)
            beside = above_now + below_now + pltpu.roll(now, 1, 1) + pltpu.roll(now, wide - 1, 1)
            store(at, keep[at % tall] * now + rate[at % tall] * beside)
            above_now, now = now, below_now

    def load_turned(at):
        picks = [
            turned[block, pl.ds(place(at), SUBLANES, stride=tall), :] for block in range(blocks)
        ]
        return jnp.concatenate(picks, 1)

    def store_result(at, value):
        for block in range(tile_cols // 128):
            result[block, pl.ds(result_place(at), SUBLANES, stride=tile_rows), :] = value[:, block * 128 : (block + 1) * 128]

    def through(buffer):
        def load(at):
            return buffer[at % tall]

        def store(at, value):
            buffer[at % tall] = value

        return load, store

    def add_member(slot):
        y_arrival(slot)
        for pair in range(pairs):
            for at, member in enumerate(widened(slot, pair)):
                slab = 2 * pair + at
                field = member * probe_field[slab]
                for block in range(blocks):
                    turned[block, slab * tall : (slab + 1) * tall] = field[:, block * 128 : (block + 1) * 128]
        load_a, store_a = through(field_a)
        load_b, store_b = through(field_b)
        loads_now = load_turned
        for step in range(SWEEPS):
            store_now = store_result if step == SWEEPS - 1 else (store_a, store_b)[step % 2]
            sweep(loads_now, store_now, SWEEPS - 1 - step)
            loads_now = (load_a, load_b)[step % 2]
        for pair in range(pairs):
            for at, member in enumerate(centre(slot, pair)):
                slab = 2 * pair + at
                done = jnp.concatenate(
                    [result[block, slab * tile_rows : (slab + 1) * tile_rows] for block in range(tile_cols // 128)], 1
                )
                total[slab] += member * done

    def hand_on(slot, part, onward):
        z_copy(slot, part, onward).wait_recv()

        @if_sent(4 + onward)
        def _():
            z_copy(slot, part, onward).start()

        if part:
            start_rows(slot)

    def at_distance(away, act):
        @pl.when(me - away >= 0)
        def _():
            act(me - away, 1)

        @pl.when(me + away < n)
        def _():
            act(me + away, 0)

    def arrivals(away):
        for part in range(len(parts)):
            at_distance(away, lambda slot, onward: hand_on(slot, part, onward))

    lower = 1 - (2 * me) // n
    ahead = has_prev + has_next

    @pl.when(ahead == 2)
    def _():
        arrivals(1)

    @pl.loop(0, 2 * n)
    def _(turn):
        away = turn // 2
        second = turn % 2
        slot = me + away * (2 * ((second + lower) % 2) - 1)

        @pl.when(second == 1)
        def _():
            arrivals(away + ahead)

        @pl.when((slot >= 0) & (slot < n) & (turn > 0))
        def _():
            add_member(slot)

    for slab in range(slabs):
        ends, middle = total[slab, :half], swap(total[slab, half:])
        out[slab, :half] = jnp.where(low_rows, ends, middle)
        out[slab, half:] = jnp.where(low_rows, middle, ends)

    @pl.loop(0, n)
    def _(slot):
        for at in range(2):
            @pl.when((sides[4 + at][0] == 1) & ((slot >= me) if at == 0 else (slot <= me)))
            def _(at=at):
                for part in range(len(parts)):
                    z_copy(slot, part, at).wait_send()

    @pl.loop(0, n + 1)
    def _(slot):
        for at in range(2):
            @if_sent(at)
            def _(at=at):
                y_copy(slot, at).wait_send()

    for at in range(2):
        @if_sent(at)
        def _(at=at):
            cy_copy(at).wait_send()

        @if_sent(2 + at)
        def _(at=at):
            for copy in x_copies(at):
                copy.wait_send()


def body(n, rows, cols, pert, probes, diff_class, class_rate):
    mem_local, variables, levels, tile_rows, tile_cols = pert.shape
    slabs = variables * levels
    pairs = slabs // 2
    half = tile_rows // 2
    wide = tile_cols + 128
    tall = tile_rows + half
    bf16 = jnp.bfloat16
    flat = (slabs, tile_rows, tile_cols)
    vmem = pl.BlockSpec(memory_space=pltpu.VMEM)
    dma = pltpu.SemaphoreType.DMA
    out = pl.pallas_call(
        functools.partial(kernel, n, rows, cols),
        out_shape=pltpu.VMEM(flat, F32),
        in_specs=[pl.BlockSpec(memory_space=pltpu.HBM)] * 4,
        out_specs=vmem,
        scratch_shapes=[
            pltpu.VMEM(flat, bf16),
            pltpu.VMEM(flat, bf16),
            pltpu.VMEM((tile_rows, tile_cols), jnp.int32),
            pltpu.SMEM(class_rate.shape, F32),
            pltpu.VMEM((n + 1, (4 * pairs + 1) * tile_rows, tile_cols // 2), bf16),
            pltpu.VMEM((n + 1, (pairs + 1) * tile_rows, tile_cols // 2), bf16),
            pltpu.VMEM((n + 1, (pairs + 1) * tile_rows, tile_cols // 2), bf16),
            pltpu.VMEM((2, 2, tile_rows, 128), bf16),
            pltpu.VMEM((2, 2, tile_rows, 128), bf16),
            pltpu.VMEM((tile_rows, wide), jnp.int32),
            pltpu.VMEM((2, tile_rows, 128), jnp.int32),
            pltpu.VMEM((half, wide), jnp.int32),
            pltpu.VMEM((half, wide), jnp.int32),
            pltpu.VMEM((slabs, tall, wide), F32),
            pltpu.VMEM((tall, SUBLANES, wide), F32),
            pltpu.VMEM((tall, SUBLANES, wide), F32),
            pltpu.VMEM((wide // 128, SUBLANES * tall, 128), F32),
            pltpu.VMEM((tall, SUBLANES, wide), F32),
            pltpu.VMEM((tall, SUBLANES, wide), F32),
            pltpu.VMEM((tile_cols // 128, SUBLANES * tile_rows, 128), F32),
            pltpu.VMEM(flat, F32),
            dma((4,)), dma((n, 2, 2)), dma((n, 2)), dma((n + 1, 2)), dma((n + 1, 2)),
            dma((2,)), dma((2,)), dma((2,)), dma((2,)), dma((2,)), dma((2,)),
        ],
        compiler_params=pltpu.CompilerParams(
            collective_id=0, has_side_effects=True, vmem_limit_bytes=60 * 1024 * 1024
        ),
    )(pert.reshape(flat), probes.reshape(flat), diff_class, class_rate)
    return out.reshape(pert.shape) / (n - 1)


def solution(mesh):
    placed = (
        P("member", None, None, "row", "col"),
        P("member", None, None, "row", "col"),
        P("row", "col"),
        P(),
    )
    sizes = (mesh.shape["member"], mesh.shape["row"], mesh.shape["col"])
    return jax.shard_map(
        functools.partial(body, *sizes),
        mesh=mesh,
        in_specs=placed,
        out_specs=P("member", None, None, "row", "col"),
        check_vma=False,
    )
```

```python
import functools

import jax
import jax.numpy as jnp
from jax import lax
from jax.experimental import pallas as pl
from jax.experimental.pallas import tpu as pltpu
from jax.sharding import PartitionSpec as P

SWEEPS = 4
SUBLANES = 8
MESH = pl.DeviceIdType.MESH
F32 = jnp.float32


def kernel(
    n, rows, cols,
    pert_hbm, probes_hbm, classes_hbm, rates_hbm, out,
    pert, probes, classes, rates,
    core, above, below,
    side_out, side_in, cls, cls_in, cls_above, cls_below,
    probe_field, keep, rate, turned, field_a, field_b, result, total,
    in_sem, z_send, z_recv, y_send, y_recv,
    x_send, x_recv, cx_send, cx_recv, cy_send, cy_recv,
):
    slabs, tile_rows, tile_cols = pert.shape
    pairs = slabs // 2
    half = tile_rows // 2
    wide = tile_cols + 128
    tall = tile_rows + half
    me = lax.axis_index("member")
    row = lax.axis_index("row")
    col = lax.axis_index("col")

    loads = [
        pltpu.make_async_copy(src, dst, in_sem.at[at])
        for at, (src, dst) in enumerate(
            ((pert_hbm, pert), (probes_hbm, probes), (classes_hbm, classes), (rates_hbm, rates))
        )
    ]
    for load in loads:
        load.start()

    has_up = (row + rows - 1) // rows
    has_down = 1 - (row + 1) // rows
    has_left = (col + cols - 1) // cols
    has_right = 1 - (col + 1) // cols
    has_prev = (me + n - 1) // n
    has_next = 1 - (me + 1) // n
    sides = (
        (has_up, {"row": row - 1}),
        (has_down, {"row": row + 1}),
        (has_left, {"col": col - 1}),
        (has_right, {"col": col + 1}),
        (has_prev, {"member": me - 1}),
        (has_next, {"member": me + 1}),
    )

    barrier = pltpu.get_barrier_semaphore()
    for has, where in sides:
        @pl.when(has == 1)
        def _(where=where):
            pl.semaphore_signal(barrier, inc=1, device_id=where, device_id_type=MESH)

    def remote(src, dst, send, recv, where):
        return pltpu.make_async_remote_copy(
            src_ref=src, dst_ref=dst, send_sem=send, recv_sem=recv,
            device_id=where, device_id_type=MESH,
        )

    def x_copies(at):
        where = sides[2 + at][1]
        block = (0, tile_cols - 128)[at]
        return (
            remote(side_out.at[at], side_in.at[at], x_send.at[at], x_recv.at[at], where),
            remote(classes.at[:, block : block + 128], cls_in.at[at], cx_send.at[at], cx_recv.at[at], where),
        )

    side_at = pairs * tile_rows
    bottom_at = side_at + tile_rows
    middle_at = bottom_at + side_at
    parts = (pl.ds(middle_at, slabs * tile_rows), pl.ds(0, middle_at))
    halo = side_at + tile_rows

    def z_copy(slot, part, at):
        return remote(
            core.at[slot, parts[part]], core.at[slot, parts[part]],
            z_send.at[slot, part, at], z_recv.at[slot, part], sides[4 + at][1],
        )

    def y_copy(slot, at):
        return remote(
            core.at[slot, pl.ds((0, side_at)[at], halo)], (below, above)[at].at[slot],
            y_send.at[slot, at], y_recv.at[slot, at], sides[at][1],
        )

    def cy_copy(at):
        return remote(
            cls.at[at * half : (at + 1) * half], (cls_below, cls_above)[at],
            cy_send.at[at], cy_recv.at[at], sides[at][1],
        )

    def if_sent(at):
        return pl.when(sides[at][0] == 1)

    fold = tile_cols // 2
    low_rows = lax.broadcasted_iota(jnp.int32, (half, tile_cols), 0) < half // 2
    low_side = lax.broadcasted_iota(jnp.int32, (half, 128), 0) < half // 2

    def swap(rows_now):
        return pltpu.roll(rows_now, half // 2, 0)

    def keep_block(slot, first, rows_now):
        both = jnp.concatenate([rows_now[:, :fold], rows_now[:, fold:]], 0)
        core[slot, first : first + tile_rows] = both.astype(jnp.bfloat16)

    def block_of(ref, slot, first):
        both = ref[slot, first : first + tile_rows].astype(F32)
        return jnp.concatenate([both[:half], both[half:]], 1)

    def pack(which, slot):
        for pair in range(pairs):
            first = which[2 * pair].astype(F32)
            second = which[2 * pair + 1].astype(F32)
            keep_block(slot, tile_rows * pair, jnp.where(low_rows, first[:half], swap(second[:half])))
            keep_block(slot, bottom_at + tile_rows * pair, jnp.where(low_rows, swap(first[half:]), second[half:]))
            for at, tile in enumerate((first, second)):
                keep_block(slot, middle_at + tile_rows * (2 * pair + at), jnp.where(low_rows, swap(tile[:half]), swap(tile[half:])))

    def start_rows(slot):
        for at in range(2):
            @if_sent(at)
            def _(at=at):
                y_copy(slot, at).start()

    for load in loads:
        load.wait()
    lane = lax.broadcasted_iota(jnp.int32, (tile_rows, 128), 1)
    for at, which in enumerate((pert, probes)):
        to_left = jnp.zeros((tile_rows, 128), F32)
        to_right = jnp.zeros((tile_rows, 128), F32)
        for slab in range(slabs):
            low = SWEEPS * slab
            head = which[slab, :, 0:128].astype(F32)
            tail = which[slab, :, tile_cols - 128 : tile_cols].astype(F32)
            if slab:
                head = pltpu.roll(head, low, 1)
                tail = pltpu.roll(tail, 128 - low, 1)
            to_left = jnp.where((lane >= low) & (lane < low + SWEEPS), head, to_left)
            to_right = jnp.where((lane >= 128 - SWEEPS - low) & (lane < 128 - low), tail, to_right)
        for way, rim in enumerate((to_left, to_right)):
            ends = jnp.where(low_side, rim[:half], rim[half:])
            middle = jnp.where(low_side, swap(rim[:half]), swap(rim[half:]))
            side_out[way, at] = jnp.concatenate([ends, middle], 0).astype(jnp.bfloat16)
    pack(pert, me)
    pl.semaphore_wait(barrier, has_up + has_down + has_left + has_right + has_prev + has_next)

    for at in range(2):
        @if_sent(2 + at)
        def _(at=at):
            for copy in x_copies(at):
                copy.start()

    for at in range(2):
        @if_sent(4 + at)
        def _(at=at):
            z_copy(me, 0, at).start()

    pack(probes, n)
    cls[:, 0:tile_cols] = classes[...]

    @pl.when(has_up == 0)
    def _():
        above[...] = jnp.zeros_like(above)
        cls_above[...] = jnp.full_like(cls_above, -1)

    @pl.when(has_down == 0)
    def _():
        below[...] = jnp.zeros_like(below)
        cls_below[...] = jnp.full_like(cls_below, -1)

    @pl.when(has_right == 0)
    def _():
        side_in[0] = jnp.zeros_like(side_in[0])
        cls_in[0] = jnp.full_like(cls_in[0], -1)

    @pl.when(has_left == 0)
    def _():
        side_in[1] = jnp.zeros_like(side_in[1])
        cls_in[1] = jnp.full_like(cls_in[1], -1)

    for at in range(2):
        @if_sent(3 - at)
        def _(at=at):
            for copy in x_copies(at):
                copy.wait_recv()

    for at, slot in enumerate((me, n)):
        merged = jnp.where(lane < 64, side_in[0, at].astype(F32), side_in[1, at].astype(F32))
        core[slot, side_at:bottom_at] = jnp.concatenate([merged] * (fold // 128), 1).astype(jnp.bfloat16)

    for at in range(2):
        @if_sent(4 + at)
        def _(at=at):
            z_copy(me, 1, at).start()
    start_rows(n)
    start_rows(me)

    cls[:, tile_cols:wide] = jnp.where(lane < 64, cls_in[0], cls_in[1])
    for at in range(2):
        @if_sent(at)
        def _(at=at):
            cy_copy(at).start()

    lane_tall = lax.broadcasted_iota(jnp.int32, (tall, 128), 1) < 64

    def place(at):
        return at + half if at < 0 else at if at < half // 2 else at + half // 2

    def top_of(slot, pair):
        return block_of(core, slot, tile_rows * pair)

    def bottom_of(slot, pair):
        return block_of(core, slot, bottom_at + tile_rows * pair)

    def middle_of(slot, pair, at):
        return block_of(core, slot, middle_at + tile_rows * (2 * pair + at))

    def widened(slot, pair):
        top, bottom = top_of(slot, pair), bottom_of(slot, pair)
        over = block_of(above, slot, tile_rows * (1 + pair))
        under = block_of(below, slot, tile_rows * pair)
        beside_own = core[slot, side_at:bottom_at, 0:128].astype(F32)
        ends, middle = beside_own[:half], beside_own[half:]
        beside = jnp.concatenate(
            [
                jnp.where(low_side, ends, above[slot, 0:tile_rows, 0:128].astype(F32)[:half]),
                middle,
                swap(jnp.where(low_side, below[slot, side_at:halo, 0:128].astype(F32)[:half], ends)),
            ],
            0,
        )
        both = []
        for at in range(2):
            low = SWEEPS * (2 * pair + at)
            if at == 0:
                head = jnp.where(low_rows, top, swap(over))
                tail = jnp.where(low_rows, bottom, swap(under))
            else:
                head = jnp.where(low_rows, swap(top), over)
                tail = jnp.where(low_rows, swap(bottom), under)
            mine = jnp.concatenate([head, middle_of(slot, pair, at), tail], 0)
            end = jnp.where(
                lane_tall,
                pltpu.roll(beside, (128 - low) % 128, 1) if low else beside,
                pltpu.roll(beside, low, 1) if low else beside,
            )
            both.append(jnp.concatenate([mine, end], 1))
        return both

    def centre(slot, pair):
        top, bottom = top_of(slot, pair), bottom_of(slot, pair)
        return [
            jnp.concatenate([ends, middle_of(slot, pair, at)], 0)
            for at, ends in enumerate(
                (jnp.where(low_rows, top, swap(bottom)), jnp.where(low_rows, swap(top), bottom))
            )
        ]

    def result_place(at):
        if at < half // 2:
            return at
        return at - half if at >= tile_rows - half // 2 else at + half // 2

    def y_arrival(slot):
        for at in range(2):
            @if_sent(1 - at)
            def _(at=at):
                y_copy(slot, at).wait_recv()

    for at in range(2):
        @if_sent(1 - at)
        def _(at=at):
            cy_copy(at).wait_recv()

    low_cls = lax.broadcasted_iota(jnp.int32, (half, wide), 0) < half // 2
    kind = jnp.concatenate([cls[...], jnp.where(low_cls, cls_below[...], cls_above[...])], 0)
    picked = jnp.zeros((tall, wide), F32)
    for level in range(rates.shape[0]):
        picked = jnp.where(kind == level, rates[level], picked)
    for at in range(tall):
        line = jnp.broadcast_to(picked[at : at + 1], (SUBLANES, wide))
        rate[at] = line
        keep[at] = 1.0 - 4.0 * line

    y_arrival(n)
    for pair in range(pairs):
        for at, field in enumerate(widened(n, pair)):
            probe_field[2 * pair + at] = field
            total[2 * pair + at] = jnp.zeros((tile_rows, tile_cols), F32)

    blocks = wide // 128
    if slabs < SUBLANES:
        turned[:, slabs * tall :] = jnp.zeros((blocks, (SUBLANES - slabs) * tall, 128), F32)

    def sweep(load, store, margin):
        above_now, now = load(-margin - 1), load(-margin)
        for at in range(-margin, tile_rows + margin):
            below_now = load(at + 1)
            beside = above_now + below_now + pltpu.roll(now, 1, 1) + pltpu.roll(now, wide - 1, 1)
            store(at, keep[at % tall] * now + rate[at % tall] * beside)
            above_now, now = now, below_now

    def load_turned(at):
        picks = [
            turned[block, pl.ds(place(at), SUBLANES, stride=tall), :] for block in range(blocks)
        ]
        return jnp.concatenate(picks, 1)

    def store_result(at, value):
        for block in range(tile_cols // 128):
            result[block, pl.ds(result_place(at), SUBLANES, stride=tile_rows), :] = value[:, block * 128 : (block + 1) * 128]

    def through(buffer):
        def load(at):
            return buffer[at % tall]

        def store(at, value):
            buffer[at % tall] = value

        return load, store

    def add_member(slot):
        y_arrival(slot)
        for pair in range(pairs):
            for at, member in enumerate(widened(slot, pair)):
                slab = 2 * pair + at
                field = member * probe_field[slab]
                for block in range(blocks):
                    turned[block, slab * tall : (slab + 1) * tall] = field[:, block * 128 : (block + 1) * 128]
        load_a, store_a = through(field_a)
        load_b, store_b = through(field_b)
        loads_now = load_turned
        for step in range(SWEEPS):
            store_now = store_result if step == SWEEPS - 1 else (store_a, store_b)[step % 2]
            sweep(loads_now, store_now, SWEEPS - 1 - step)
            loads_now = (load_a, load_b)[step % 2]
        for pair in range(pairs):
            for at, member in enumerate(centre(slot, pair)):
                slab = 2 * pair + at
                done = jnp.concatenate(
                    [result[block, slab * tile_rows : (slab + 1) * tile_rows] for block in range(tile_cols // 128)], 1
                )
                total[slab] += member * done

    def hand_on(slot, part, onward):
        z_copy(slot, part, onward).wait_recv()

        @if_sent(4 + onward)
        def _():
            z_copy(slot, part, onward).start()

        if part:
            start_rows(slot)

    def at_distance(away, act):
        @pl.when(me - away >= 0)
        def _():
            act(me - away, 1)

        @pl.when(me + away < n)
        def _():
            act(me + away, 0)

    def arrivals(away):
        for part in range(len(parts)):
            at_distance(away, lambda slot, onward: hand_on(slot, part, onward))

    lower = 1 - (2 * me) // n
    ahead = has_prev + has_next

    @pl.when(ahead == 2)
    def _():
        arrivals(1)

    @pl.loop(0, 2 * n)
    def _(turn):
        away = turn // 2
        second = turn % 2
        slot = me + away * (1 - 2 * ((second + lower) % 2))

        @pl.when(second == 1)
        def _():
            arrivals(away + ahead)

        @pl.when((slot >= 0) & (slot < n) & (turn > 0))
        def _():
            add_member(slot)

    for slab in range(slabs):
        ends, middle = total[slab, :half], swap(total[slab, half:])
        out[slab, :half] = jnp.where(low_rows, ends, middle)
        out[slab, half:] = jnp.where(low_rows, middle, ends)

    @pl.loop(0, n)
    def _(slot):
        for at in range(2):
            @pl.when((sides[4 + at][0] == 1) & ((slot >= me) if at == 0 else (slot <= me)))
            def _(at=at):
                for part in range(len(parts)):
                    z_copy(slot, part, at).wait_send()

    @pl.loop(0, n + 1)
    def _(slot):
        for at in range(2):
            @if_sent(at)
            def _(at=at):
                y_copy(slot, at).wait_send()

    for at in range(2):
        @if_sent(at)
        def _(at=at):
            cy_copy(at).wait_send()

        @if_sent(2 + at)
        def _(at=at):
            for copy in x_copies(at):
                copy.wait_send()


def body(n, rows, cols, pert, probes, diff_class, class_rate):
    mem_local, variables, levels, tile_rows, tile_cols = pert.shape
    slabs = variables * levels
    pairs = slabs // 2
    half = tile_rows // 2
    wide = tile_cols + 128
    tall = tile_rows + half
    bf16 = jnp.bfloat16
    flat = (slabs, tile_rows, tile_cols)
    vmem = pl.BlockSpec(memory_space=pltpu.VMEM)
    dma = pltpu.SemaphoreType.DMA
    out = pl.pallas_call(
        functools.partial(kernel, n, rows, cols),
        out_shape=pltpu.VMEM(flat, F32),
        in_specs=[pl.BlockSpec(memory_space=pltpu.HBM)] * 4,
        out_specs=vmem,
        scratch_shapes=[
            pltpu.VMEM(flat, bf16),
            pltpu.VMEM(flat, bf16),
            pltpu.VMEM((tile_rows, tile_cols), jnp.int32),
            pltpu.SMEM(class_rate.shape, F32),
            pltpu.VMEM((n + 1, (4 * pairs + 1) * tile_rows, tile_cols // 2), bf16),
            pltpu.VMEM((n + 1, (pairs + 1) * tile_rows, tile_cols // 2), bf16),
            pltpu.VMEM((n + 1, (pairs + 1) * tile_rows, tile_cols // 2), bf16),
            pltpu.VMEM((2, 2, tile_rows, 128), bf16),
            pltpu.VMEM((2, 2, tile_rows, 128), bf16),
            pltpu.VMEM((tile_rows, wide), jnp.int32),
            pltpu.VMEM((2, tile_rows, 128), jnp.int32),
            pltpu.VMEM((half, wide), jnp.int32),
            pltpu.VMEM((half, wide), jnp.int32),
            pltpu.VMEM((slabs, tall, wide), F32),
            pltpu.VMEM((tall, SUBLANES, wide), F32),
            pltpu.VMEM((tall, SUBLANES, wide), F32),
            pltpu.VMEM((wide // 128, SUBLANES * tall, 128), F32),
            pltpu.VMEM((tall, SUBLANES, wide), F32),
            pltpu.VMEM((tall, SUBLANES, wide), F32),
            pltpu.VMEM((tile_cols // 128, SUBLANES * tile_rows, 128), F32),
            pltpu.VMEM(flat, F32),
            dma((4,)), dma((n, 2, 2)), dma((n, 2)), dma((n + 1, 2)), dma((n + 1, 2)),
            dma((2,)), dma((2,)), dma((2,)), dma((2,)), dma((2,)), dma((2,)),
        ],
        compiler_params=pltpu.CompilerParams(
            collective_id=0, has_side_effects=True, vmem_limit_bytes=60 * 1024 * 1024
        ),
    )(pert.reshape(flat), probes.reshape(flat), diff_class, class_rate)
    return out.reshape(pert.shape) / (n - 1)


def solution(mesh):
    placed = (
        P("member", None, None, "row", "col"),
        P("member", None, None, "row", "col"),
        P("row", "col"),
        P(),
    )
    sizes = (mesh.shape["member"], mesh.shape["row"], mesh.shape["col"])
    return jax.shard_map(
        functools.partial(body, *sizes),
        mesh=mesh,
        in_specs=placed,
        out_specs=P("member", None, None, "row", "col"),
        check_vma=False,
    )
```

```python
import functools

import jax
import jax.numpy as jnp
from jax import lax
from jax.experimental import pallas as pl
from jax.experimental.pallas import tpu as pltpu
from jax.sharding import PartitionSpec as P

SWEEPS = 4
SUBLANES = 8
MESH = pl.DeviceIdType.MESH
F32 = jnp.float32


def kernel(
    n, rows, cols,
    pert_hbm, probes_hbm, classes_hbm, rates_hbm, out,
    pert, probes, classes, rates,
    core, above, below,
    side_out, side_in, cls, cls_in, cls_above, cls_below,
    probe_field, keep, rate, turned, field_a, field_b, result, total,
    in_sem, z_send, z_far, z_recv, y_send, y_recv,
    x_send, x_recv, cx_send, cx_recv, cy_send, cy_recv,
):
    slabs, tile_rows, tile_cols = pert.shape
    pairs = slabs // 2
    half = tile_rows // 2
    wide = tile_cols + 128
    tall = tile_rows + half
    me = lax.axis_index("member")
    row = lax.axis_index("row")
    col = lax.axis_index("col")

    loads = [
        pltpu.make_async_copy(src, dst, in_sem.at[at])
        for at, (src, dst) in enumerate(
            ((pert_hbm, pert), (probes_hbm, probes), (classes_hbm, classes), (rates_hbm, rates))
        )
    ]
    for load in loads:
        load.start()

    has_up = (row + rows - 1) // rows
    has_down = 1 - (row + 1) // rows
    has_left = (col + cols - 1) // cols
    has_right = 1 - (col + 1) // cols
    has_prev = (me + n - 1) // n
    has_next = 1 - (me + 1) // n
    has_prev2 = (me + n - 2) // n
    has_next2 = 1 - (me + 2) // n
    sides = (
        (has_up, {"row": row - 1}),
        (has_down, {"row": row + 1}),
        (has_left, {"col": col - 1}),
        (has_right, {"col": col + 1}),
        (has_prev, {"member": me - 1}),
        (has_next, {"member": me + 1}),
        (has_prev2, {"member": me - 2}),
        (has_next2, {"member": me + 2}),
    )

    barrier = pltpu.get_barrier_semaphore()
    for has, where in sides:
        @pl.when(has == 1)
        def _(where=where):
            pl.semaphore_signal(barrier, inc=1, device_id=where, device_id_type=MESH)

    def remote(src, dst, send, recv, where):
        return pltpu.make_async_remote_copy(
            src_ref=src, dst_ref=dst, send_sem=send, recv_sem=recv,
            device_id=where, device_id_type=MESH,
        )

    def x_copies(at):
        where = sides[2 + at][1]
        block = (0, tile_cols - 128)[at]
        return (
            remote(side_out.at[at], side_in.at[at], x_send.at[at], x_recv.at[at], where),
            remote(classes.at[:, block : block + 128], cls_in.at[at], cx_send.at[at], cx_recv.at[at], where),
        )

    side_at = pairs * tile_rows
    bottom_at = side_at + tile_rows
    middle_at = bottom_at + side_at
    parts = (pl.ds(middle_at, slabs * tile_rows), pl.ds(0, middle_at))
    halo = side_at + tile_rows

    def z_copy(slot, part, at):
        return remote(
            core.at[slot, parts[part]], core.at[slot, parts[part]],
            z_send.at[slot, part, at], z_recv.at[slot, part], sides[4 + at][1],
        )

    def z_far_copy(part, at):
        return remote(
            core.at[me, parts[part]], core.at[me, parts[part]],
            z_far.at[part, at], z_recv.at[me, part], sides[6 + at][1],
        )

    def z_start(part):
        for at in range(2):
            @if_sent(6 + at)
            def _(at=at):
                z_far_copy(part, at).start()
        for at in range(2):
            @if_sent(4 + at)
            def _(at=at):
                z_copy(me, part, at).start()

    def y_copy(slot, at):
        return remote(
            core.at[slot, pl.ds((0, side_at)[at], halo)], (below, above)[at].at[slot],
            y_send.at[slot, at], y_recv.at[slot, at], sides[at][1],
        )

    def cy_copy(at):
        return remote(
            cls.at[at * half : (at + 1) * half], (cls_below, cls_above)[at],
            cy_send.at[at], cy_recv.at[at], sides[at][1],
        )

    def if_sent(at):
        return pl.when(sides[at][0] == 1)

    fold = tile_cols // 2
    low_rows = lax.broadcasted_iota(jnp.int32, (half, tile_cols), 0) < half // 2
    low_side = lax.broadcasted_iota(jnp.int32, (half, 128), 0) < half // 2

    def swap(rows_now):
        return pltpu.roll(rows_now, half // 2, 0)

    def keep_block(slot, first, rows_now):
        both = jnp.concatenate([rows_now[:, :fold], rows_now[:, fold:]], 0)
        core[slot, first : first + tile_rows] = both.astype(jnp.bfloat16)

    def block_of(ref, slot, first):
        both = ref[slot, first : first + tile_rows].astype(F32)
        return jnp.concatenate([both[:half], both[half:]], 1)

    def pack(which, slot):
        for pair in range(pairs):
            first = which[2 * pair].astype(F32)
            second = which[2 * pair + 1].astype(F32)
            keep_block(slot, tile_rows * pair, jnp.where(low_rows, first[:half], swap(second[:half])))
            keep_block(slot, bottom_at + tile_rows * pair, jnp.where(low_rows, swap(first[half:]), second[half:]))
            for at, tile in enumerate((first, second)):
                keep_block(slot, middle_at + tile_rows * (2 * pair + at), jnp.where(low_rows, swap(tile[:half]), swap(tile[half:])))

    def start_rows(slot):
        for at in range(2):
            @if_sent(at)
            def _(at=at):
                y_copy(slot, at).start()

    for load in loads:
        load.wait()
    lane = lax.broadcasted_iota(jnp.int32, (tile_rows, 128), 1)
    for at, which in enumerate((pert, probes)):
        to_left = jnp.zeros((tile_rows, 128), F32)
        to_right = jnp.zeros((tile_rows, 128), F32)
        for slab in range(slabs):
            low = SWEEPS * slab
            head = which[slab, :, 0:128].astype(F32)
            tail = which[slab, :, tile_cols - 128 : tile_cols].astype(F32)
            if slab:
                head = pltpu.roll(head, low, 1)
                tail = pltpu.roll(tail, 128 - low, 1)
            to_left = jnp.where((lane >= low) & (lane < low + SWEEPS), head, to_left)
            to_right = jnp.where((lane >= 128 - SWEEPS - low) & (lane < 128 - low), tail, to_right)
        for way, rim in enumerate((to_left, to_right)):
            ends = jnp.where(low_side, rim[:half], rim[half:])
            middle = jnp.where(low_side, swap(rim[:half]), swap(rim[half:]))
            side_out[way, at] = jnp.concatenate([ends, middle], 0).astype(jnp.bfloat16)
    pack(pert, me)
    pl.semaphore_wait(barrier, has_up + has_down + has_left + has_right + has_prev + has_next + has_prev2 + has_next2)

    for at in range(2):
        @if_sent(2 + at)
        def _(at=at):
            for copy in x_copies(at):
                copy.start()

    z_start(0)

    pack(probes, n)
    cls[:, 0:tile_cols] = classes[...]

    @pl.when(has_up == 0)
    def _():
        above[...] = jnp.zeros_like(above)
        cls_above[...] = jnp.full_like(cls_above, -1)

    @pl.when(has_down == 0)
    def _():
        below[...] = jnp.zeros_like(below)
        cls_below[...] = jnp.full_like(cls_below, -1)

    @pl.when(has_right == 0)
    def _():
        side_in[0] = jnp.zeros_like(side_in[0])
        cls_in[0] = jnp.full_like(cls_in[0], -1)

    @pl.when(has_left == 0)
    def _():
        side_in[1] = jnp.zeros_like(side_in[1])
        cls_in[1] = jnp.full_like(cls_in[1], -1)

    for at in range(2):
        @if_sent(3 - at)
        def _(at=at):
            for copy in x_copies(at):
                copy.wait_recv()

    for at, slot in enumerate((me, n)):
        merged = jnp.where(lane < 64, side_in[0, at].astype(F32), side_in[1, at].astype(F32))
        core[slot, side_at:bottom_at] = jnp.concatenate([merged] * (fold // 128), 1).astype(jnp.bfloat16)

    z_start(1)
    start_rows(n)
    start_rows(me)

    cls[:, tile_cols:wide] = jnp.where(lane < 64, cls_in[0], cls_in[1])
    for at in range(2):
        @if_sent(at)
        def _(at=at):
            cy_copy(at).start()

    lane_tall = lax.broadcasted_iota(jnp.int32, (tall, 128), 1) < 64

    def place(at):
        return at + half if at < 0 else at if at < half // 2 else at + half // 2

    def top_of(slot, pair):
        return block_of(core, slot, tile_rows * pair)

    def bottom_of(slot, pair):
        return block_of(core, slot, bottom_at + tile_rows * pair)

    def middle_of(slot, pair, at):
        return block_of(core, slot, middle_at + tile_rows * (2 * pair + at))

    def widened(slot, pair):
        top, bottom = top_of(slot, pair), bottom_of(slot, pair)
        over = block_of(above, slot, tile_rows * (1 + pair))
        under = block_of(below, slot, tile_rows * pair)
        beside_own = core[slot, side_at:bottom_at, 0:128].astype(F32)
        ends, middle = beside_own[:half], beside_own[half:]
        beside = jnp.concatenate(
            [
                jnp.where(low_side, ends, above[slot, 0:tile_rows, 0:128].astype(F32)[:half]),
                middle,
                swap(jnp.where(low_side, below[slot, side_at:halo, 0:128].astype(F32)[:half], ends)),
            ],
            0,
        )
        both = []
        for at in range(2):
            low = SWEEPS * (2 * pair + at)
            if at == 0:
                head = jnp.where(low_rows, top, swap(over))
                tail = jnp.where(low_rows, bottom, swap(under))
            else:
                head = jnp.where(low_rows, swap(top), over)
                tail = jnp.where(low_rows, swap(bottom), under)
            mine = jnp.concatenate([head, middle_of(slot, pair, at), tail], 0)
            end = jnp.where(
                lane_tall,
                pltpu.roll(beside, (128 - low) % 128, 1) if low else beside,
                pltpu.roll(beside, low, 1) if low else beside,
            )
            both.append(jnp.concatenate([mine, end], 1))
        return both

    def centre(slot, pair):
        top, bottom = top_of(slot, pair), bottom_of(slot, pair)
        return [
            jnp.concatenate([ends, middle_of(slot, pair, at)], 0)
            for at, ends in enumerate(
                (jnp.where(low_rows, top, swap(bottom)), jnp.where(low_rows, swap(top), bottom))
            )
        ]

    def result_place(at):
        if at < half // 2:
            return at
        return at - half if at >= tile_rows - half // 2 else at + half // 2

    def y_arrival(slot):
        for at in range(2):
            @if_sent(1 - at)
            def _(at=at):
                y_copy(slot, at).wait_recv()

    for at in range(2):
        @if_sent(1 - at)
        def _(at=at):
            cy_copy(at).wait_recv()

    low_cls = lax.broadcasted_iota(jnp.int32, (half, wide), 0) < half // 2
    kind = jnp.concatenate([cls[...], jnp.where(low_cls, cls_below[...], cls_above[...])], 0)
    picked = jnp.zeros((tall, wide), F32)
    for level in range(rates.shape[0]):
        picked = jnp.where(kind == level, rates[level], picked)
    for at in range(tall):
        line = jnp.broadcast_to(picked[at : at + 1], (SUBLANES, wide))
        rate[at] = line
        keep[at] = 1.0 - 4.0 * line

    y_arrival(n)
    for pair in range(pairs):
        for at, field in enumerate(widened(n, pair)):
            probe_field[2 * pair + at] = field
            total[2 * pair + at] = jnp.zeros((tile_rows, tile_cols), F32)

    blocks = wide // 128
    if slabs < SUBLANES:
        turned[:, slabs * tall :] = jnp.zeros((blocks, (SUBLANES - slabs) * tall, 128), F32)

    def sweep(load, store, margin):
        above_now, now = load(-margin - 1), load(-margin)
        for at in range(-margin, tile_rows + margin):
            below_now = load(at + 1)
            beside = above_now + below_now + pltpu.roll(now, 1, 1) + pltpu.roll(now, wide - 1, 1)
            store(at, keep[at % tall] * now + rate[at % tall] * beside)
            above_now, now = now, below_now

    def load_turned(at):
        picks = [
            turned[block, pl.ds(place(at), SUBLANES, stride=tall), :] for block in range(blocks)
        ]
        return jnp.concatenate(picks, 1)

    def store_result(at, value):
        for block in range(tile_cols // 128):
            result[block, pl.ds(result_place(at), SUBLANES, stride=tile_rows), :] = value[:, block * 128 : (block + 1) * 128]

    def through(buffer):
        def load(at):
            return buffer[at % tall]

        def store(at, value):
            buffer[at % tall] = value

        return load, store

    def add_member(slot):
        y_arrival(slot)
        for pair in range(pairs):
            for at, member in enumerate(widened(slot, pair)):
                slab = 2 * pair + at
                field = member * probe_field[slab]
                for block in range(blocks):
                    turned[block, slab * tall : (slab + 1) * tall] = field[:, block * 128 : (block + 1) * 128]
        load_a, store_a = through(field_a)
        load_b, store_b = through(field_b)
        loads_now = load_turned
        for step in range(SWEEPS):
            store_now = store_result if step == SWEEPS - 1 else (store_a, store_b)[step % 2]
            sweep(loads_now, store_now, SWEEPS - 1 - step)
            loads_now = (load_a, load_b)[step % 2]
        for pair in range(pairs):
            for at, member in enumerate(centre(slot, pair)):
                slab = 2 * pair + at
                done = jnp.concatenate(
                    [result[block, slab * tile_rows : (slab + 1) * tile_rows] for block in range(tile_cols // 128)], 1
                )
                total[slab] += member * done

    def hand_on(slot, part, onward, away):
        z_copy(slot, part, onward).wait_recv()

        @pl.when((sides[4 + onward][0] == 1) & (away >= 2))
        def _():
            z_copy(slot, part, onward).start()

        if part:
            start_rows(slot)

    def at_distance(away, act):
        @pl.when(me - away >= 0)
        def _():
            act(me - away, 1)

        @pl.when(me + away < n)
        def _():
            act(me + away, 0)

    def arrivals(away):
        for part in range(len(parts)):
            at_distance(away, lambda slot, onward: hand_on(slot, part, onward, away))

    lower = 1 - (2 * me) // n
    ahead = has_prev + has_next

    @pl.when(ahead == 2)
    def _():
        arrivals(1)

    @pl.loop(0, 2 * n)
    def _(turn):
        away = turn // 2
        second = turn % 2
        slot = me + away * (1 - 2 * ((second + lower) % 2))

        @pl.when(second == 1)
        def _():
            arrivals(away + ahead)

        @pl.when((slot >= 0) & (slot < n) & (turn > 0))
        def _():
            add_member(slot)

    for slab in range(slabs):
        ends, middle = total[slab, :half], swap(total[slab, half:])
        out[slab, :half] = jnp.where(low_rows, ends, middle)
        out[slab, half:] = jnp.where(low_rows, middle, ends)

    @pl.loop(0, n)
    def _(slot):
        for at in range(2):
            @pl.when(
                (sides[4 + at][0] == 1)
                & ((slot == me) | ((slot >= me + 2) if at == 0 else (slot <= me - 2)))
            )
            def _(at=at):
                for part in range(len(parts)):
                    z_copy(slot, part, at).wait_send()

    for at in range(2):
        @if_sent(6 + at)
        def _(at=at):
            for part in range(len(parts)):
                z_far_copy(part, at).wait_send()

    @pl.loop(0, n + 1)
    def _(slot):
        for at in range(2):
            @if_sent(at)
            def _(at=at):
                y_copy(slot, at).wait_send()

    for at in range(2):
        @if_sent(at)
        def _(at=at):
            cy_copy(at).wait_send()

        @if_sent(2 + at)
        def _(at=at):
            for copy in x_copies(at):
                copy.wait_send()


def body(n, rows, cols, pert, probes, diff_class, class_rate):
    mem_local, variables, levels, tile_rows, tile_cols = pert.shape
    slabs = variables * levels
    pairs = slabs // 2
    half = tile_rows // 2
    wide = tile_cols + 128
    tall = tile_rows + half
    bf16 = jnp.bfloat16
    flat = (slabs, tile_rows, tile_cols)
    vmem = pl.BlockSpec(memory_space=pltpu.VMEM)
    dma = pltpu.SemaphoreType.DMA
    out = pl.pallas_call(
        functools.partial(kernel, n, rows, cols),
        out_shape=pltpu.VMEM(flat, F32),
        in_specs=[pl.BlockSpec(memory_space=pltpu.HBM)] * 4,
        out_specs=vmem,
        scratch_shapes=[
            pltpu.VMEM(flat, bf16),
            pltpu.VMEM(flat, bf16),
            pltpu.VMEM((tile_rows, tile_cols), jnp.int32),
            pltpu.SMEM(class_rate.shape, F32),
            pltpu.VMEM((n + 1, (4 * pairs + 1) * tile_rows, tile_cols // 2), bf16),
            pltpu.VMEM((n + 1, (pairs + 1) * tile_rows, tile_cols // 2), bf16),
            pltpu.VMEM((n + 1, (pairs + 1) * tile_rows, tile_cols // 2), bf16),
            pltpu.VMEM((2, 2, tile_rows, 128), bf16),
            pltpu.VMEM((2, 2, tile_rows, 128), bf16),
            pltpu.VMEM((tile_rows, wide), jnp.int32),
            pltpu.VMEM((2, tile_rows, 128), jnp.int32),
            pltpu.VMEM((half, wide), jnp.int32),
            pltpu.VMEM((half, wide), jnp.int32),
            pltpu.VMEM((slabs, tall, wide), F32),
            pltpu.VMEM((tall, SUBLANES, wide), F32),
            pltpu.VMEM((tall, SUBLANES, wide), F32),
            pltpu.VMEM((wide // 128, SUBLANES * tall, 128), F32),
            pltpu.VMEM((tall, SUBLANES, wide), F32),
            pltpu.VMEM((tall, SUBLANES, wide), F32),
            pltpu.VMEM((tile_cols // 128, SUBLANES * tile_rows, 128), F32),
            pltpu.VMEM(flat, F32),
            dma((4,)), dma((n, 2, 2)), dma((2, 2)), dma((n, 2)), dma((n + 1, 2)), dma((n + 1, 2)),
            dma((2,)), dma((2,)), dma((2,)), dma((2,)), dma((2,)), dma((2,)),
        ],
        compiler_params=pltpu.CompilerParams(
            collective_id=0, has_side_effects=True, vmem_limit_bytes=60 * 1024 * 1024
        ),
    )(pert.reshape(flat), probes.reshape(flat), diff_class, class_rate)
    return out.reshape(pert.shape) / (n - 1)


def solution(mesh):
    placed = (
        P("member", None, None, "row", "col"),
        P("member", None, None, "row", "col"),
        P("row", "col"),
        P(),
    )
    sizes = (mesh.shape["member"], mesh.shape["row"], mesh.shape["col"])
    return jax.shard_map(
        functools.partial(body, *sizes),
        mesh=mesh,
        in_specs=placed,
        out_specs=P("member", None, None, "row", "col"),
        check_vma=False,
    )
```

```python
import functools

import jax
import jax.numpy as jnp
from jax import lax
from jax.experimental import pallas as pl
from jax.experimental.pallas import tpu as pltpu
from jax.sharding import PartitionSpec as P

SWEEPS = 4
SUBLANES = 8
MESH = pl.DeviceIdType.MESH
F32 = jnp.float32


def kernel(
    n, rows, cols,
    pert_hbm, probes_hbm, classes_hbm, rates_hbm, out,
    pert, probes, classes, rates,
    core, above, below,
    side_out, side_in, cls, cls_in, cls_above, cls_below,
    probe_field, keep, rate, turned, field_a, field_b, result, total,
    in_sem, z_send, z_far, z_recv, y_send, y_recv,
    x_send, x_recv, cx_send, cx_recv, cy_send, cy_recv,
):
    slabs, tile_rows, tile_cols = pert.shape
    pairs = slabs // 2
    half = tile_rows // 2
    wide = tile_cols + 128
    tall = tile_rows + half
    me = lax.axis_index("member")
    row = lax.axis_index("row")
    col = lax.axis_index("col")

    loads = [
        pltpu.make_async_copy(src, dst, in_sem.at[at])
        for at, (src, dst) in enumerate(
            ((pert_hbm, pert), (probes_hbm, probes), (classes_hbm, classes), (rates_hbm, rates))
        )
    ]
    for load in loads:
        load.start()

    has_up = (row + rows - 1) // rows
    has_down = 1 - (row + 1) // rows
    has_left = (col + cols - 1) // cols
    has_right = 1 - (col + 1) // cols
    has_prev = (me + n - 1) // n
    has_next = 1 - (me + 1) // n
    has_prev2 = (me + n - 2) // n
    has_next2 = 1 - (me + 2) // n
    sides = (
        (has_up, {"row": row - 1}),
        (has_down, {"row": row + 1}),
        (has_left, {"col": col - 1}),
        (has_right, {"col": col + 1}),
        (has_prev, {"member": me - 1}),
        (has_next, {"member": me + 1}),
        (has_prev2, {"member": me - 2}),
        (has_next2, {"member": me + 2}),
    )

    barrier = pltpu.get_barrier_semaphore()
    for has, where in sides:
        @pl.when(has == 1)
        def _(where=where):
            pl.semaphore_signal(barrier, inc=1, device_id=where, device_id_type=MESH)

    def remote(src, dst, send, recv, where):
        return pltpu.make_async_remote_copy(
            src_ref=src, dst_ref=dst, send_sem=send, recv_sem=recv,
            device_id=where, device_id_type=MESH,
        )

    def x_copies(at):
        where = sides[2 + at][1]
        block = (0, tile_cols - 128)[at]
        return (
            remote(side_out.at[at], side_in.at[at], x_send.at[at], x_recv.at[at], where),
            remote(classes.at[:, block : block + 128], cls_in.at[at], cx_send.at[at], cx_recv.at[at], where),
        )

    side_at = pairs * tile_rows
    bottom_at = side_at + tile_rows
    middle_at = bottom_at + side_at
    parts = (pl.ds(middle_at, slabs * tile_rows), pl.ds(0, middle_at))
    halo = side_at + tile_rows

    def z_copy(slot, part, at):
        return remote(
            core.at[slot, parts[part]], core.at[slot, parts[part]],
            z_send.at[slot, part, at], z_recv.at[slot, part], sides[4 + at][1],
        )

    def z_far_copy(part, at):
        return remote(
            core.at[me, parts[part]], core.at[me, parts[part]],
            z_far.at[part, at], z_recv.at[me, part], sides[6 + at][1],
        )

    def z_start(part):
        for at in range(2):
            @if_sent(6 + at)
            def _(at=at):
                z_far_copy(part, at).start()
        for at in range(2):
            @if_sent(4 + at)
            def _(at=at):
                z_copy(me, part, at).start()

    def y_copy(slot, at):
        return remote(
            core.at[slot, pl.ds((0, side_at)[at], halo)], (below, above)[at].at[slot],
            y_send.at[slot, at], y_recv.at[slot, at], sides[at][1],
        )

    def cy_copy(at):
        return remote(
            cls.at[at * half : (at + 1) * half], (cls_below, cls_above)[at],
            cy_send.at[at], cy_recv.at[at], sides[at][1],
        )

    def if_sent(at):
        return pl.when(sides[at][0] == 1)

    fold = tile_cols // 2
    low_rows = lax.broadcasted_iota(jnp.int32, (half, tile_cols), 0) < half // 2
    low_side = lax.broadcasted_iota(jnp.int32, (half, 128), 0) < half // 2

    def swap(rows_now):
        return pltpu.roll(rows_now, half // 2, 0)

    def keep_block(slot, first, rows_now):
        both = jnp.concatenate([rows_now[:, :fold], rows_now[:, fold:]], 0)
        core[slot, first : first + tile_rows] = both.astype(jnp.bfloat16)

    def block_of(ref, slot, first):
        both = ref[slot, first : first + tile_rows].astype(F32)
        return jnp.concatenate([both[:half], both[half:]], 1)

    def pack(which, slot):
        for pair in range(pairs):
            first = which[2 * pair].astype(F32)
            second = which[2 * pair + 1].astype(F32)
            keep_block(slot, tile_rows * pair, jnp.where(low_rows, first[:half], swap(second[:half])))
            keep_block(slot, bottom_at + tile_rows * pair, jnp.where(low_rows, swap(first[half:]), second[half:]))
            for at, tile in enumerate((first, second)):
                keep_block(slot, middle_at + tile_rows * (2 * pair + at), jnp.where(low_rows, swap(tile[:half]), swap(tile[half:])))

    def start_rows(slot):
        for at in range(2):
            @if_sent(at)
            def _(at=at):
                y_copy(slot, at).start()

    for load in loads:
        load.wait()
    lane = lax.broadcasted_iota(jnp.int32, (tile_rows, 128), 1)
    for at, which in enumerate((pert, probes)):
        to_left = jnp.zeros((tile_rows, 128), F32)
        to_right = jnp.zeros((tile_rows, 128), F32)
        for slab in range(slabs):
            low = SWEEPS * slab
            head = which[slab, :, 0:128].astype(F32)
            tail = which[slab, :, tile_cols - 128 : tile_cols].astype(F32)
            if slab:
                head = pltpu.roll(head, low, 1)
                tail = pltpu.roll(tail, 128 - low, 1)
            to_left = jnp.where((lane >= low) & (lane < low + SWEEPS), head, to_left)
            to_right = jnp.where((lane >= 128 - SWEEPS - low) & (lane < 128 - low), tail, to_right)
        for way, rim in enumerate((to_left, to_right)):
            ends = jnp.where(low_side, rim[:half], rim[half:])
            middle = jnp.where(low_side, swap(rim[:half]), swap(rim[half:]))
            side_out[way, at] = jnp.concatenate([ends, middle], 0).astype(jnp.bfloat16)
    pack(pert, me)
    pl.semaphore_wait(barrier, has_up + has_down + has_left + has_right + has_prev + has_next + has_prev2 + has_next2)

    for at in range(2):
        @if_sent(2 + at)
        def _(at=at):
            for copy in x_copies(at):
                copy.start()

    z_start(0)

    pack(probes, n)
    cls[:, 0:tile_cols] = classes[...]

    @pl.when(has_up == 0)
    def _():
        above[...] = jnp.zeros_like(above)
        cls_above[...] = jnp.full_like(cls_above, -1)

    @pl.when(has_down == 0)
    def _():
        below[...] = jnp.zeros_like(below)
        cls_below[...] = jnp.full_like(cls_below, -1)

    @pl.when(has_right == 0)
    def _():
        side_in[0] = jnp.zeros_like(side_in[0])
        cls_in[0] = jnp.full_like(cls_in[0], -1)

    @pl.when(has_left == 0)
    def _():
        side_in[1] = jnp.zeros_like(side_in[1])
        cls_in[1] = jnp.full_like(cls_in[1], -1)

    for at in range(2):
        @if_sent(3 - at)
        def _(at=at):
            for copy in x_copies(at):
                copy.wait_recv()

    for at, slot in enumerate((me, n)):
        merged = jnp.where(lane < 64, side_in[0, at].astype(F32), side_in[1, at].astype(F32))
        core[slot, side_at:bottom_at] = jnp.concatenate([merged] * (fold // 128), 1).astype(jnp.bfloat16)

    z_start(1)
    start_rows(n)
    start_rows(me)

    cls[:, tile_cols:wide] = jnp.where(lane < 64, cls_in[0], cls_in[1])
    for at in range(2):
        @if_sent(at)
        def _(at=at):
            cy_copy(at).start()

    lane_tall = lax.broadcasted_iota(jnp.int32, (tall, 128), 1) < 64

    def place(at):
        return at + half if at < 0 else at if at < half // 2 else at + half // 2

    def top_of(slot, pair):
        return block_of(core, slot, tile_rows * pair)

    def bottom_of(slot, pair):
        return block_of(core, slot, bottom_at + tile_rows * pair)

    def middle_of(slot, pair, at):
        return block_of(core, slot, middle_at + tile_rows * (2 * pair + at))

    def widened(slot, pair):
        top, bottom = top_of(slot, pair), bottom_of(slot, pair)
        over = block_of(above, slot, tile_rows * (1 + pair))
        under = block_of(below, slot, tile_rows * pair)
        beside_own = core[slot, side_at:bottom_at, 0:128].astype(F32)
        ends, middle = beside_own[:half], beside_own[half:]
        beside = jnp.concatenate(
            [
                jnp.where(low_side, ends, above[slot, 0:tile_rows, 0:128].astype(F32)[:half]),
                middle,
                swap(jnp.where(low_side, below[slot, side_at:halo, 0:128].astype(F32)[:half], ends)),
            ],
            0,
        )
        both = []
        for at in range(2):
            low = SWEEPS * (2 * pair + at)
            if at == 0:
                head = jnp.where(low_rows, top, swap(over))
                tail = jnp.where(low_rows, bottom, swap(under))
            else:
                head = jnp.where(low_rows, swap(top), over)
                tail = jnp.where(low_rows, swap(bottom), under)
            mine = jnp.concatenate([head, middle_of(slot, pair, at), tail], 0)
            end = jnp.where(
                lane_tall,
                pltpu.roll(beside, (128 - low) % 128, 1) if low else beside,
                pltpu.roll(beside, low, 1) if low else beside,
            )
            both.append(jnp.concatenate([mine, end], 1))
        return both

    def centre(slot, pair):
        top, bottom = top_of(slot, pair), bottom_of(slot, pair)
        return [
            jnp.concatenate([ends, middle_of(slot, pair, at)], 0)
            for at, ends in enumerate(
                (jnp.where(low_rows, top, swap(bottom)), jnp.where(low_rows, swap(top), bottom))
            )
        ]

    def result_place(at):
        if at < half // 2:
            return at
        return at - half if at >= tile_rows - half // 2 else at + half // 2

    def y_arrival(slot):
        for at in range(2):
            @if_sent(1 - at)
            def _(at=at):
                y_copy(slot, at).wait_recv()

    for at in range(2):
        @if_sent(1 - at)
        def _(at=at):
            cy_copy(at).wait_recv()

    low_cls = lax.broadcasted_iota(jnp.int32, (half, wide), 0) < half // 2
    kind = jnp.concatenate([cls[...], jnp.where(low_cls, cls_below[...], cls_above[...])], 0)
    picked = jnp.zeros((tall, wide), F32)
    for level in range(rates.shape[0]):
        picked = jnp.where(kind == level, rates[level], picked)
    for at in range(tall):
        line = jnp.broadcast_to(picked[at : at + 1], (SUBLANES, wide))
        rate[at] = line
        keep[at] = 1.0 - 4.0 * line

    y_arrival(n)
    for pair in range(pairs):
        for at, field in enumerate(widened(n, pair)):
            probe_field[2 * pair + at] = field
            total[2 * pair + at] = jnp.zeros((tile_rows, tile_cols), F32)

    blocks = wide // 128
    if slabs < SUBLANES:
        turned[:, slabs * tall :] = jnp.zeros((blocks, (SUBLANES - slabs) * tall, 128), F32)

    def sweep(load, store, margin):
        above_now, now = load(-margin - 1), load(-margin)
        for at in range(-margin, tile_rows + margin):
            below_now = load(at + 1)
            beside = above_now + below_now + pltpu.roll(now, 1, 1) + pltpu.roll(now, wide - 1, 1)
            store(at, keep[at % tall] * now + rate[at % tall] * beside)
            above_now, now = now, below_now

    def load_turned(at):
        picks = [
            turned[block, pl.ds(place(at), SUBLANES, stride=tall), :] for block in range(blocks)
        ]
        return jnp.concatenate(picks, 1)

    def store_result(at, value):
        for block in range(tile_cols // 128):
            result[block, pl.ds(result_place(at), SUBLANES, stride=tile_rows), :] = value[:, block * 128 : (block + 1) * 128]

    def through(buffer):
        def load(at):
            return buffer[at % tall]

        def store(at, value):
            buffer[at % tall] = value

        return load, store

    def add_member(slot):
        y_arrival(slot)
        for pair in range(pairs):
            for at, member in enumerate(widened(slot, pair)):
                slab = 2 * pair + at
                field = member * probe_field[slab]
                for block in range(blocks):
                    turned[block, slab * tall : (slab + 1) * tall] = field[:, block * 128 : (block + 1) * 128]
        load_a, store_a = through(field_a)
        load_b, store_b = through(field_b)
        loads_now = load_turned
        for step in range(SWEEPS):
            store_now = store_result if step == SWEEPS - 1 else (store_a, store_b)[step % 2]
            sweep(loads_now, store_now, SWEEPS - 1 - step)
            loads_now = (load_a, load_b)[step % 2]
        for pair in range(pairs):
            for at, member in enumerate(centre(slot, pair)):
                slab = 2 * pair + at
                done = jnp.concatenate(
                    [result[block, slab * tile_rows : (slab + 1) * tile_rows] for block in range(tile_cols // 128)], 1
                )
                total[slab] += member * done

    def hand_on(slot, part, onward, away):
        z_copy(slot, part, onward).wait_recv()

        @pl.when((sides[4 + onward][0] == 1) & (away >= 2))
        def _():
            z_copy(slot, part, onward).start()

        if part:
            start_rows(slot)

    def at_distance(away, act):
        @pl.when(me - away >= 0)
        def _():
            act(me - away, 1)

        @pl.when(me + away < n)
        def _():
            act(me + away, 0)

    def arrivals(away):
        for part in range(len(parts)):
            at_distance(away, lambda slot, onward: hand_on(slot, part, onward, away))

    lower = 1 - (2 * me) // n

    @pl.loop(0, 2 * n)
    def _(turn):
        away = turn // 2
        second = turn % 2
        slot = me + away * (1 - 2 * ((second + lower) % 2))

        @pl.when(second == 0)
        def _():
            arrivals(away + 1)

        @pl.when((slot >= 0) & (slot < n) & (turn > 0))
        def _():
            add_member(slot)

    for slab in range(slabs):
        ends, middle = total[slab, :half], swap(total[slab, half:])
        out[slab, :half] = jnp.where(low_rows, ends, middle)
        out[slab, half:] = jnp.where(low_rows, middle, ends)

    @pl.loop(0, n)
    def _(slot):
        for at in range(2):
            @pl.when(
                (sides[4 + at][0] == 1)
                & ((slot == me) | ((slot >= me + 2) if at == 0 else (slot <= me - 2)))
            )
            def _(at=at):
                for part in range(len(parts)):
                    z_copy(slot, part, at).wait_send()

    for at in range(2):
        @if_sent(6 + at)
        def _(at=at):
            for part in range(len(parts)):
                z_far_copy(part, at).wait_send()

    @pl.loop(0, n + 1)
    def _(slot):
        for at in range(2):
            @if_sent(at)
            def _(at=at):
                y_copy(slot, at).wait_send()

    for at in range(2):
        @if_sent(at)
        def _(at=at):
            cy_copy(at).wait_send()

        @if_sent(2 + at)
        def _(at=at):
            for copy in x_copies(at):
                copy.wait_send()


def body(n, rows, cols, pert, probes, diff_class, class_rate):
    mem_local, variables, levels, tile_rows, tile_cols = pert.shape
    slabs = variables * levels
    pairs = slabs // 2
    half = tile_rows // 2
    wide = tile_cols + 128
    tall = tile_rows + half
    bf16 = jnp.bfloat16
    flat = (slabs, tile_rows, tile_cols)
    vmem = pl.BlockSpec(memory_space=pltpu.VMEM)
    dma = pltpu.SemaphoreType.DMA
    out = pl.pallas_call(
        functools.partial(kernel, n, rows, cols),
        out_shape=pltpu.VMEM(flat, F32),
        in_specs=[pl.BlockSpec(memory_space=pltpu.HBM)] * 4,
        out_specs=vmem,
        scratch_shapes=[
            pltpu.VMEM(flat, bf16),
            pltpu.VMEM(flat, bf16),
            pltpu.VMEM((tile_rows, tile_cols), jnp.int32),
            pltpu.SMEM(class_rate.shape, F32),
            pltpu.VMEM((n + 1, (4 * pairs + 1) * tile_rows, tile_cols // 2), bf16),
            pltpu.VMEM((n + 1, (pairs + 1) * tile_rows, tile_cols // 2), bf16),
            pltpu.VMEM((n + 1, (pairs + 1) * tile_rows, tile_cols // 2), bf16),
            pltpu.VMEM((2, 2, tile_rows, 128), bf16),
            pltpu.VMEM((2, 2, tile_rows, 128), bf16),
            pltpu.VMEM((tile_rows, wide), jnp.int32),
            pltpu.VMEM((2, tile_rows, 128), jnp.int32),
            pltpu.VMEM((half, wide), jnp.int32),
            pltpu.VMEM((half, wide), jnp.int32),
            pltpu.VMEM((slabs, tall, wide), F32),
            pltpu.VMEM((tall, SUBLANES, wide), F32),
            pltpu.VMEM((tall, SUBLANES, wide), F32),
            pltpu.VMEM((wide // 128, SUBLANES * tall, 128), F32),
            pltpu.VMEM((tall, SUBLANES, wide), F32),
            pltpu.VMEM((tall, SUBLANES, wide), F32),
            pltpu.VMEM((tile_cols // 128, SUBLANES * tile_rows, 128), F32),
            pltpu.VMEM(flat, F32),
            dma((4,)), dma((n, 2, 2)), dma((2, 2)), dma((n, 2)), dma((n + 1, 2)), dma((n + 1, 2)),
            dma((2,)), dma((2,)), dma((2,)), dma((2,)), dma((2,)), dma((2,)),
        ],
        compiler_params=pltpu.CompilerParams(
            collective_id=0, has_side_effects=True, vmem_limit_bytes=60 * 1024 * 1024
        ),
    )(pert.reshape(flat), probes.reshape(flat), diff_class, class_rate)
    return out.reshape(pert.shape) / (n - 1)


def solution(mesh):
    placed = (
        P("member", None, None, "row", "col"),
        P("member", None, None, "row", "col"),
        P("row", "col"),
        P(),
    )
    sizes = (mesh.shape["member"], mesh.shape["row"], mesh.shape["col"])
    return jax.shard_map(
        functools.partial(body, *sizes),
        mesh=mesh,
        in_specs=placed,
        out_specs=P("member", None, None, "row", "col"),
        check_vma=False,
    )
```

```python
import functools

import jax
import jax.numpy as jnp
from jax import lax
from jax.experimental import pallas as pl
from jax.experimental.pallas import tpu as pltpu
from jax.sharding import PartitionSpec as P

SWEEPS = 4
SUBLANES = 8
MESH = pl.DeviceIdType.MESH
F32 = jnp.float32


def kernel(
    n, rows, cols,
    pert_hbm, probes_hbm, classes_hbm, rates_hbm, out,
    pert, probes, classes, rates,
    core, above, below,
    side_out, side_in, cls, cls_in, cls_above, cls_below,
    probe_field, keep, rate, turned, field_a, field_b, result, total,
    in_sem, z_send, z_far, z_recv, y_send, y_recv,
    x_send, x_recv, cx_send, cx_recv, cy_send, cy_recv,
):
    slabs, tile_rows, tile_cols = pert.shape
    pairs = slabs // 2
    half = tile_rows // 2
    wide = tile_cols + 128
    tall = tile_rows + half
    me = lax.axis_index("member")
    row = lax.axis_index("row")
    col = lax.axis_index("col")

    loads = [
        pltpu.make_async_copy(src, dst, in_sem.at[at])
        for at, (src, dst) in enumerate(
            ((pert_hbm, pert), (probes_hbm, probes), (classes_hbm, classes), (rates_hbm, rates))
        )
    ]
    for load in loads:
        load.start()

    has_up = (row + rows - 1) // rows
    has_down = 1 - (row + 1) // rows
    has_left = (col + cols - 1) // cols
    has_right = 1 - (col + 1) // cols
    has_prev = (me + n - 1) // n
    has_next = 1 - (me + 1) // n
    has_prev2 = (me + n - 2) // n
    has_next2 = 1 - (me + 2) // n
    sides = (
        (has_up, {"row": row - 1}),
        (has_down, {"row": row + 1}),
        (has_left, {"col": col - 1}),
        (has_right, {"col": col + 1}),
        (has_prev, {"member": me - 1}),
        (has_next, {"member": me + 1}),
        (has_prev2, {"member": me - 2}),
        (has_next2, {"member": me + 2}),
    )

    barrier = pltpu.get_barrier_semaphore()
    for has, where in sides:
        @pl.when(has == 1)
        def _(where=where):
            pl.semaphore_signal(barrier, inc=1, device_id=where, device_id_type=MESH)

    def remote(src, dst, send, recv, where):
        return pltpu.make_async_remote_copy(
            src_ref=src, dst_ref=dst, send_sem=send, recv_sem=recv,
            device_id=where, device_id_type=MESH,
        )

    def x_copies(at):
        where = sides[2 + at][1]
        block = (0, tile_cols - 128)[at]
        return (
            remote(side_out.at[at], side_in.at[at], x_send.at[at], x_recv.at[at], where),
            remote(classes.at[:, block : block + 128], cls_in.at[at], cx_send.at[at], cx_recv.at[at], where),
        )

    side_at = pairs * tile_rows
    bottom_at = side_at + tile_rows
    middle_at = bottom_at + side_at
    parts = (pl.ds(middle_at, slabs * tile_rows), pl.ds(0, middle_at))
    halo = side_at + tile_rows

    def z_copy(slot, part, at):
        return remote(
            core.at[slot, parts[part]], core.at[slot, parts[part]],
            z_send.at[slot, part, at], z_recv.at[slot, part], sides[4 + at][1],
        )

    def z_far_copy(part, at):
        return remote(
            core.at[me, parts[part]], core.at[me, parts[part]],
            z_far.at[part, at], z_recv.at[me, part], sides[6 + at][1],
        )

    def z_start(part):
        for at in range(2):
            @if_sent(6 + at)
            def _(at=at):
                z_far_copy(part, at).start()
        for at in range(2):
            @if_sent(4 + at)
            def _(at=at):
                z_copy(me, part, at).start()

    def y_copy(slot, at):
        return remote(
            core.at[slot, pl.ds((0, side_at)[at], halo)], (below, above)[at].at[slot],
            y_send.at[slot, at], y_recv.at[slot, at], sides[at][1],
        )

    def cy_copy(at):
        return remote(
            cls.at[at * half : (at + 1) * half], (cls_below, cls_above)[at],
            cy_send.at[at], cy_recv.at[at], sides[at][1],
        )

    def if_sent(at):
        return pl.when(sides[at][0] == 1)

    fold = tile_cols // 2
    low_rows = lax.broadcasted_iota(jnp.int32, (half, tile_cols), 0) < half // 2
    low_side = lax.broadcasted_iota(jnp.int32, (half, 128), 0) < half // 2

    def swap(rows_now):
        return pltpu.roll(rows_now, half // 2, 0)

    def keep_block(slot, first, rows_now):
        both = jnp.concatenate([rows_now[:, :fold], rows_now[:, fold:]], 0)
        core[slot, first : first + tile_rows] = both.astype(jnp.bfloat16)

    def block_of(ref, slot, first):
        both = ref[slot, first : first + tile_rows].astype(F32)
        return jnp.concatenate([both[:half], both[half:]], 1)

    def pack(which, slot):
        for pair in range(pairs):
            first = which[2 * pair].astype(F32)
            second = which[2 * pair + 1].astype(F32)
            keep_block(slot, tile_rows * pair, jnp.where(low_rows, first[:half], swap(second[:half])))
            keep_block(slot, bottom_at + tile_rows * pair, jnp.where(low_rows, swap(first[half:]), second[half:]))
            for at, tile in enumerate((first, second)):
                keep_block(slot, middle_at + tile_rows * (2 * pair + at), jnp.where(low_rows, swap(tile[:half]), swap(tile[half:])))

    def start_rows(slot):
        for at in range(2):
            @if_sent(at)
            def _(at=at):
                y_copy(slot, at).start()

    for load in loads:
        load.wait()
    lane = lax.broadcasted_iota(jnp.int32, (tile_rows, 128), 1)
    for at, which in enumerate((pert, probes)):
        to_left = jnp.zeros((tile_rows, 128), F32)
        to_right = jnp.zeros((tile_rows, 128), F32)
        for slab in range(slabs):
            low = SWEEPS * slab
            head = which[slab, :, 0:128].astype(F32)
            tail = which[slab, :, tile_cols - 128 : tile_cols].astype(F32)
            if slab:
                head = pltpu.roll(head, low, 1)
                tail = pltpu.roll(tail, 128 - low, 1)
            to_left = jnp.where((lane >= low) & (lane < low + SWEEPS), head, to_left)
            to_right = jnp.where((lane >= 128 - SWEEPS - low) & (lane < 128 - low), tail, to_right)
        for way, rim in enumerate((to_left, to_right)):
            ends = jnp.where(low_side, rim[:half], rim[half:])
            middle = jnp.where(low_side, swap(rim[:half]), swap(rim[half:]))
            side_out[way, at] = jnp.concatenate([ends, middle], 0).astype(jnp.bfloat16)
    pack(pert, me)
    pl.semaphore_wait(barrier, has_up + has_down + has_left + has_right + has_prev + has_next + has_prev2 + has_next2)

    for at in range(2):
        @if_sent(2 + at)
        def _(at=at):
            for copy in x_copies(at):
                copy.start()

    z_start(0)

    pack(probes, n)
    cls[:, 0:tile_cols] = classes[...]

    @pl.when(has_up == 0)
    def _():
        above[...] = jnp.zeros_like(above)
        cls_above[...] = jnp.full_like(cls_above, -1)

    @pl.when(has_down == 0)
    def _():
        below[...] = jnp.zeros_like(below)
        cls_below[...] = jnp.full_like(cls_below, -1)

    @pl.when(has_right == 0)
    def _():
        side_in[0] = jnp.zeros_like(side_in[0])
        cls_in[0] = jnp.full_like(cls_in[0], -1)

    @pl.when(has_left == 0)
    def _():
        side_in[1] = jnp.zeros_like(side_in[1])
        cls_in[1] = jnp.full_like(cls_in[1], -1)

    for at in range(2):
        @if_sent(3 - at)
        def _(at=at):
            for copy in x_copies(at):
                copy.wait_recv()

    for at, slot in enumerate((me, n)):
        merged = jnp.where(lane < 64, side_in[0, at].astype(F32), side_in[1, at].astype(F32))
        core[slot, side_at:bottom_at] = jnp.concatenate([merged] * (fold // 128), 1).astype(jnp.bfloat16)

    z_start(1)
    start_rows(n)
    start_rows(me)

    cls[:, tile_cols:wide] = jnp.where(lane < 64, cls_in[0], cls_in[1])
    for at in range(2):
        @if_sent(at)
        def _(at=at):
            cy_copy(at).start()

    lane_tall = lax.broadcasted_iota(jnp.int32, (tall, 128), 1) < 64

    def place(at):
        return at + half if at < 0 else at if at < half // 2 else at + half // 2

    def top_of(slot, pair):
        return block_of(core, slot, tile_rows * pair)

    def bottom_of(slot, pair):
        return block_of(core, slot, bottom_at + tile_rows * pair)

    def middle_of(slot, pair, at):
        return block_of(core, slot, middle_at + tile_rows * (2 * pair + at))

    def widened(slot, pair):
        top, bottom = top_of(slot, pair), bottom_of(slot, pair)
        over = block_of(above, slot, tile_rows * (1 + pair))
        under = block_of(below, slot, tile_rows * pair)
        beside_own = core[slot, side_at:bottom_at, 0:128].astype(F32)
        ends, middle = beside_own[:half], beside_own[half:]
        beside = jnp.concatenate(
            [
                jnp.where(low_side, ends, above[slot, 0:tile_rows, 0:128].astype(F32)[:half]),
                middle,
                swap(jnp.where(low_side, below[slot, side_at:halo, 0:128].astype(F32)[:half], ends)),
            ],
            0,
        )
        both = []
        for at in range(2):
            low = SWEEPS * (2 * pair + at)
            if at == 0:
                head = jnp.where(low_rows, top, swap(over))
                tail = jnp.where(low_rows, bottom, swap(under))
            else:
                head = jnp.where(low_rows, swap(top), over)
                tail = jnp.where(low_rows, swap(bottom), under)
            mine = jnp.concatenate([head, middle_of(slot, pair, at), tail], 0)
            end = jnp.where(
                lane_tall,
                pltpu.roll(beside, (128 - low) % 128, 1) if low else beside,
                pltpu.roll(beside, low, 1) if low else beside,
            )
            both.append(jnp.concatenate([mine, end], 1))
        return both

    def centre(slot, pair):
        top, bottom = top_of(slot, pair), bottom_of(slot, pair)
        return [
            jnp.concatenate([ends, middle_of(slot, pair, at)], 0)
            for at, ends in enumerate(
                (jnp.where(low_rows, top, swap(bottom)), jnp.where(low_rows, swap(top), bottom))
            )
        ]

    def result_place(at):
        if at < half // 2:
            return at
        return at - half if at >= tile_rows - half // 2 else at + half // 2

    def y_arrival(slot):
        for at in range(2):
            @if_sent(1 - at)
            def _(at=at):
                y_copy(slot, at).wait_recv()

    for at in range(2):
        @if_sent(1 - at)
        def _(at=at):
            cy_copy(at).wait_recv()

    low_cls = lax.broadcasted_iota(jnp.int32, (half, wide), 0) < half // 2
    kind = jnp.concatenate([cls[...], jnp.where(low_cls, cls_below[...], cls_above[...])], 0)
    picked = jnp.zeros((tall, wide), F32)
    for level in range(rates.shape[0]):
        picked = jnp.where(kind == level, rates[level], picked)
    for at in range(tall):
        line = jnp.broadcast_to(picked[at : at + 1], (SUBLANES, wide))
        rate[at] = line
        keep[at] = 1.0 - 4.0 * line

    y_arrival(n)
    for pair in range(pairs):
        for at, field in enumerate(widened(n, pair)):
            probe_field[2 * pair + at] = field
            total[2 * pair + at] = jnp.zeros((tile_rows, tile_cols), F32)

    blocks = wide // 128
    if slabs < SUBLANES:
        turned[:, slabs * tall :] = jnp.zeros((blocks, (SUBLANES - slabs) * tall, 128), F32)

    def sweep(load, store, margin):
        above_now, now = load(-margin - 1), load(-margin)
        for at in range(-margin, tile_rows + margin):
            below_now = load(at + 1)
            beside = above_now + below_now + pltpu.roll(now, 1, 1) + pltpu.roll(now, wide - 1, 1)
            store(at, keep[at % tall] * now + rate[at % tall] * beside)
            above_now, now = now, below_now

    def load_turned(at):
        picks = [
            turned[block, pl.ds(place(at), SUBLANES, stride=tall), :] for block in range(blocks)
        ]
        return jnp.concatenate(picks, 1)

    def store_result(at, value):
        for block in range(tile_cols // 128):
            result[block, pl.ds(result_place(at), SUBLANES, stride=tile_rows), :] = value[:, block * 128 : (block + 1) * 128]

    def through(buffer):
        def load(at):
            return buffer[at % tall]

        def store(at, value):
            buffer[at % tall] = value

        return load, store

    def add_member(slot):
        y_arrival(slot)
        for pair in range(pairs):
            for at, member in enumerate(widened(slot, pair)):
                slab = 2 * pair + at
                field = member * probe_field[slab]
                for block in range(blocks):
                    turned[block, slab * tall : (slab + 1) * tall] = field[:, block * 128 : (block + 1) * 128]
        load_a, store_a = through(field_a)
        load_b, store_b = through(field_b)
        loads_now = load_turned
        for step in range(SWEEPS):
            store_now = store_result if step == SWEEPS - 1 else (store_a, store_b)[step % 2]
            sweep(loads_now, store_now, SWEEPS - 1 - step)
            loads_now = (load_a, load_b)[step % 2]
        for pair in range(pairs):
            for at, member in enumerate(centre(slot, pair)):
                slab = 2 * pair + at
                done = jnp.concatenate(
                    [result[block, slab * tile_rows : (slab + 1) * tile_rows] for block in range(tile_cols // 128)], 1
                )
                total[slab] += member * done

    def hand_on(slot, part, onward, away):
        z_copy(slot, part, onward).wait_recv()

        @pl.when((sides[4 + onward][0] == 1) & (away >= 2))
        def _():
            z_copy(slot, part, onward).start()

        if part:
            start_rows(slot)

    def at_distance(away, act):
        @pl.when(me - away >= 0)
        def _():
            act(me - away, 1)

        @pl.when(me + away < n)
        def _():
            act(me + away, 0)

    def arrivals(away):
        for part in range(len(parts)):
            at_distance(away, lambda slot, onward: hand_on(slot, part, onward, away))

    lower = 1 - (2 * me) // n
    ahead = has_prev + has_next

    @pl.when(ahead == 2)
    def _():
        arrivals(1)

    @pl.loop(0, 2 * n)
    def _(turn):
        away = turn // 2
        second = turn % 2
        slot = me + away * (1 - 2 * ((second + lower) % 2))

        early = (second == 1) & ((ahead == 2) | (away != n - 2))
        last = (second == 0) & (ahead == 1) & (away == n - 1)

        @pl.when(early | last)
        def _():
            arrivals(away + ahead + second - 1)

        @pl.when((slot >= 0) & (slot < n) & (turn > 0))
        def _():
            add_member(slot)

    for slab in range(slabs):
        ends, middle = total[slab, :half], swap(total[slab, half:])
        out[slab, :half] = jnp.where(low_rows, ends, middle)
        out[slab, half:] = jnp.where(low_rows, middle, ends)

    @pl.loop(0, n)
    def _(slot):
        for at in range(2):
            @pl.when(
                (sides[4 + at][0] == 1)
                & ((slot == me) | ((slot >= me + 2) if at == 0 else (slot <= me - 2)))
            )
            def _(at=at):
                for part in range(len(parts)):
                    z_copy(slot, part, at).wait_send()

    for at in range(2):
        @if_sent(6 + at)
        def _(at=at):
            for part in range(len(parts)):
                z_far_copy(part, at).wait_send()

    @pl.loop(0, n + 1)
    def _(slot):
        for at in range(2):
            @if_sent(at)
            def _(at=at):
                y_copy(slot, at).wait_send()

    for at in range(2):
        @if_sent(at)
        def _(at=at):
            cy_copy(at).wait_send()

        @if_sent(2 + at)
        def _(at=at):
            for copy in x_copies(at):
                copy.wait_send()


def body(n, rows, cols, pert, probes, diff_class, class_rate):
    mem_local, variables, levels, tile_rows, tile_cols = pert.shape
    slabs = variables * levels
    pairs = slabs // 2
    half = tile_rows // 2
    wide = tile_cols + 128
    tall = tile_rows + half
    bf16 = jnp.bfloat16
    flat = (slabs, tile_rows, tile_cols)
    vmem = pl.BlockSpec(memory_space=pltpu.VMEM)
    dma = pltpu.SemaphoreType.DMA
    out = pl.pallas_call(
        functools.partial(kernel, n, rows, cols),
        out_shape=pltpu.VMEM(flat, F32),
        in_specs=[pl.BlockSpec(memory_space=pltpu.HBM)] * 4,
        out_specs=vmem,
        scratch_shapes=[
            pltpu.VMEM(flat, bf16),
            pltpu.VMEM(flat, bf16),
            pltpu.VMEM((tile_rows, tile_cols), jnp.int32),
            pltpu.SMEM(class_rate.shape, F32),
            pltpu.VMEM((n + 1, (4 * pairs + 1) * tile_rows, tile_cols // 2), bf16),
            pltpu.VMEM((n + 1, (pairs + 1) * tile_rows, tile_cols // 2), bf16),
            pltpu.VMEM((n + 1, (pairs + 1) * tile_rows, tile_cols // 2), bf16),
            pltpu.VMEM((2, 2, tile_rows, 128), bf16),
            pltpu.VMEM((2, 2, tile_rows, 128), bf16),
            pltpu.VMEM((tile_rows, wide), jnp.int32),
            pltpu.VMEM((2, tile_rows, 128), jnp.int32),
            pltpu.VMEM((half, wide), jnp.int32),
            pltpu.VMEM((half, wide), jnp.int32),
            pltpu.VMEM((slabs, tall, wide), F32),
            pltpu.VMEM((tall, SUBLANES, wide), F32),
            pltpu.VMEM((tall, SUBLANES, wide), F32),
            pltpu.VMEM((wide // 128, SUBLANES * tall, 128), F32),
            pltpu.VMEM((tall, SUBLANES, wide), F32),
            pltpu.VMEM((tall, SUBLANES, wide), F32),
            pltpu.VMEM((tile_cols // 128, SUBLANES * tile_rows, 128), F32),
            pltpu.VMEM(flat, F32),
            dma((4,)), dma((n, 2, 2)), dma((2, 2)), dma((n, 2)), dma((n + 1, 2)), dma((n + 1, 2)),
            dma((2,)), dma((2,)), dma((2,)), dma((2,)), dma((2,)), dma((2,)),
        ],
        compiler_params=pltpu.CompilerParams(
            collective_id=0, has_side_effects=True, vmem_limit_bytes=60 * 1024 * 1024
        ),
    )(pert.reshape(flat), probes.reshape(flat), diff_class, class_rate)
    return out.reshape(pert.shape) / (n - 1)


def solution(mesh):
    placed = (
        P("member", None, None, "row", "col"),
        P("member", None, None, "row", "col"),
        P("row", "col"),
        P(),
    )
    sizes = (mesh.shape["member"], mesh.shape["row"], mesh.shape["col"])
    return jax.shard_map(
        functools.partial(body, *sizes),
        mesh=mesh,
        in_specs=placed,
        out_specs=P("member", None, None, "row", "col"),
        check_vma=False,
    )
```
